32 devices in a mesh: kv: 4 (over z), blk: 8 (over y, x, core).
Axes of the slice: x: 2, y: 2, z: 4, core: 2. Of those that a mesh axis runs over, the one named last changes fastest.
Arguments:
- hidden_in: bfloat16 [4, 16, 4096], P(None, None, 'blk'), may hold values from -6 to 6
- attn_gain: bfloat16 [4096], P('blk'), may hold values from 0.5 to 1.5
- ffn_gain: bfloat16 [4096], replicated, may hold values from 0.5 to 1.5
- query_key_value_weight: bfloat16 [4096, 8, 768], P('blk', 'kv'), may hold values from -0.09375 to 0.09375
- out_weight: bfloat16 [4096, 4096], P('kv', 'blk'), may hold values from -0.09375 to 0.09375
- router_weight: bfloat16 [4096, 8], replicated, may hold values from -0.09375 to 0.09375
- expert_in: bfloat16 [8, 4096, 2, 8192], P('kv', None, None, 'blk'), may hold values from -0.09375 to 0.09375
- expert_down: bfloat16 [8, 8192, 4096], P('kv', 'blk'), may hold values from -0.09375 to 0.09375
- kv_cache: bfloat16 [2048, 2, 8, 128, 128], P('blk', None, 'kv')
- lengths: int32 [2], replicated, may hold values from 1 to 16384, as said below
- tables: int32 [16, 128], replicated, may hold values from 0 to 2047, as said below
- parents: int32 [4, 16], replicated, may hold values from 0 to 15, as said below
- routes: int32 [4, 16, 2], replicated, may hold values from 0 to 7, all different within a row; in each aligned block of 16 rows (0 to 15, 16 to 31, ..., all dimensions but the last counted through in order) at most 6 rows name the same one
Outputs:
- layer_out: bfloat16 [4, 16, 4096], P(None, None, 'blk')
The draws below stay inside these ranges and needn't reach their ends.
Inputs may be any that keep to these rules, and one draw needn't show every extreme that they name: `lengths`: one group has exactly 16384 cached positions. `tables`: each pool block is named exactly once. `parents`: a beam's parent is a beam of its own group of 8 consecutive beams. `routes`: in each step no expert is named by more than 6 beams, a bound that some block reaches.
All inputs are finite; a program needn't handle non-finite values.
Results may differ from the reference program's by a relative error of at most 0.013.
Values may be sent and summed in bfloat16 or wider, within the bound.
A program may use at most 192 MiB of HBM per device.

```python
import math
import jax
import jax.numpy as jnp
import numpy as np
from jax import lax

MODEL_WIDTH = 4096
QUERY_HEADS = 32
KEY_VALUE_HEADS = 8
HEAD_WIDTH = 128
QUERIES_PER_KEY = 4
EXPERTS = 8
FF = 8192
BEAM_W = 8
GROUPS = 2
DECODE_STEPS = 4
BLOCK_POSITIONS = 128
BEAM_BLOCKS = 128
BEAM_TOTAL = 16
CAP = 6


def draw_kv_cache(key, part):
    first_key = jax.random.fold_in(jax.random.fold_in(key, 11), 0)
    mean_key = jax.random.fold_in(jax.random.fold_in(key, 11), 2)
    pool_count = BEAM_TOTAL * BEAM_BLOCKS
    complete_shape = (pool_count, 2, KEY_VALUE_HEADS, BLOCK_POSITIONS, HEAD_WIDTH)
    selector = jnp.array([1.0, 0.0], jnp.float32).reshape(1, 2, 1, 1, 1)
    value_pick = 1.0 - selector
    mean_vector = jax.random.normal(mean_key, (1, 1, KEY_VALUE_HEADS, 1, HEAD_WIDTH), jnp.float32)
    fraction = (jnp.arange(pool_count, dtype=jnp.float32) / (pool_count - 1)).reshape(pool_count, 1, 1, 1, 1)
    ramp = 1.0 + 4.0 * fraction
    values = jax.random.normal(first_key, complete_shape, jnp.float32) + value_pick * ramp * mean_vector
    return values.astype(jnp.bfloat16)


def draw_lengths(key, part):
    first_key, following_key, third_key = jax.random.split(jax.random.fold_in(key, 29), 3)
    longest = BEAM_BLOCKS * BLOCK_POSITIONS
    base = jax.random.randint(first_key, (GROUPS,), 1, longest + 1)
    order = jax.random.permutation(following_key, GROUPS)
    other_len = jax.random.randint(third_key, (), 1, longest)
    base = base.at[order[0]].set(longest)
    base = base.at[order[1]].set(other_len)
    return base.astype(jnp.int32)


def draw_tables(key, part):
    order = jax.random.permutation(jax.random.fold_in(key, 37), BEAM_TOTAL * BEAM_BLOCKS)
    return order.reshape(BEAM_TOTAL, BEAM_BLOCKS).astype(jnp.int32)


def draw_parents(key, part):
    offsets = jax.random.randint(jax.random.fold_in(key, 41), (DECODE_STEPS, BEAM_TOTAL), 0, BEAM_W)
    group_base = jnp.arange(BEAM_TOTAL, dtype=jnp.int32) // BEAM_W * BEAM_W
    return (offsets + group_base[None, :]).astype(jnp.int32)


def spiked(entries, rng, source, target, parts, factor):
    def block_of(axis_at):
        return (jnp.arange(entries.shape[axis_at]) // (entries.shape[axis_at] // parts)).reshape((-1,) + (1,) * (entries.ndim - 1 - axis_at))

    first = jax.random.permutation(rng, parts)[block_of(target)]
    far = (block_of(target) + parts // 2) % parts
    return jnp.where((block_of(source) == first) | (block_of(source) == far), factor * entries, entries)


def block_levels(key, shape, pieces, least, largest):
    level, own = 1.0, jax.random.fold_in(key, 6)
    for dim, blocks in pieces:
        draws = jnp.exp(jax.random.uniform(jax.random.fold_in(own, dim), (blocks,), jnp.float32, least / len(pieces), largest / len(pieces)))
        level = level * jnp.repeat(draws, shape[dim] // blocks).reshape([-1 if axis == dim else 1 for axis in range(len(shape))])
    return level


def assign_block(stream_key, own, number, rows, amount, top, reach, skew):
    sequence = jax.random.permutation(stream_key, amount)
    crowded, ordinary = load_shares(amount, rows * top, reach, skew, True), load_shares(amount, rows * top, reach, skew, False)
    places = jnp.arange(amount)

    def named(sizes, rotation):
        used = int((sizes > 0).sum())
        fixed = max(1, used // 4)
        passed = fixed + (places - fixed + rotation * (used - fixed)) % max(1, amount - fixed)
        return jnp.zeros((amount,), jnp.int32).at[sequence[jnp.where(places < fixed, places, passed)]].set(jnp.asarray(sizes, jnp.int32))

    sizes = jnp.where(number % 4 == 0, named(crowded, number // 4), named(ordinary, number - number // 4 - 1))
    mixed = jax.random.permutation(jax.random.fold_in(own, 3), amount)
    donor, sink = mixed[0:amount // 2 * 2:2], mixed[1:amount // 2 * 2:2]
    margin = jnp.minimum(sizes[donor] - 1, reach - sizes[sink]) // 2
    margin = jnp.where((donor == sequence[0]) | (sink == sequence[0]) | (sizes[sink] == 0), 0, jnp.maximum(margin, 0))
    passed = jax.random.randint(jax.random.fold_in(own, 4), (amount // 2,), 0, 1 << 20) % (margin + 1)
    sizes = sizes.at[donor].add(-passed).at[sink].add(passed)
    labels = jnp.searchsorted(jnp.cumsum(sizes), jnp.arange(rows * top), side="right").astype(jnp.int32)
    listing = labels.reshape(top, rows).T
    listing = listing[jax.random.permutation(jax.random.fold_in(own, 1), rows)]
    rotation = jax.random.randint(jax.random.fold_in(own, 2), (rows, 1), 0, top)
    return jnp.take_along_axis(listing, (jnp.arange(top)[None, :] + rotation) % top, axis=1)


def load_shares(amount, total, reach, lean, full):
    weights = [(1 << 20) // math.isqrt(rank ** lean) + 1 for rank in range(1, amount + 1)]
    largest = reach if full else min(reach, max(-(-total // amount), total * weights[0] // sum(weights)))
    least = 1 if total - largest >= amount - 1 else 0
    given, spare = [largest] + [least] * (amount - 1), total - largest - least * (amount - 1)
    while spare > 0:
        free = [i for i in range(1, amount) if given[i] < largest] or [i for i in range(1, amount) if given[i] < reach]
        pool, left = sum([weights[i] for i in free]), spare
        for i in free:
            extra = min(reach - given[i], max(1, left * weights[i] // pool), spare)
            given[i] = given[i] + extra
            spare = spare - extra
    return np.array(given)


def centred(key, shape, scale, most, shards=(), kind=jnp.bfloat16):
    level = block_levels(key, shape, shards, -0.22, 0.18) if shards else 1.0
    drawn = jax.random.normal(key, shape, jnp.float32) * scale * level
    return jnp.minimum(jnp.maximum(drawn, -most), most).astype(kind)


def noise_with(own_key, extent, spread, reach, cuts, heavy, kind=jnp.bfloat16):
    values = spread * jax.random.normal(own_key, extent, jnp.float32)
    if cuts:
        values = values * block_levels(own_key, extent, cuts, -0.22, 0.18)
    return jnp.clip(spiked(values, jax.random.fold_in(own_key, 3), *heavy), -reach, reach).astype(kind)


def setup_inputs(seed: int = 0) -> dict:
    arg_keys = jax.random.split(jax.random.key(seed), 14)
    hidden_in = centred(arg_keys[0], (DECODE_STEPS, BEAM_TOTAL, MODEL_WIDTH), 1.0, 6.0, ((2, 8),))
    attn_gain = jnp.clip(1.0 + 0.1 * jax.random.normal(arg_keys[1], (MODEL_WIDTH,), jnp.float32), 0.5, 1.5).astype(jnp.bfloat16)
    ffn_gain = jnp.clip(1.0 + 0.1 * jax.random.normal(arg_keys[2], (MODEL_WIDTH,), jnp.float32), 0.5, 1.5).astype(jnp.bfloat16)
    query_key_value_weight = centred(arg_keys[3], (MODEL_WIDTH, KEY_VALUE_HEADS, (QUERY_HEADS // KEY_VALUE_HEADS + 2) * HEAD_WIDTH), MODEL_WIDTH ** -0.5, 0.09375, ((0, 8), (1, 4)))
    out_weight = centred(arg_keys[4], (QUERY_HEADS * HEAD_WIDTH, MODEL_WIDTH), (QUERY_HEADS * HEAD_WIDTH) ** -0.5, 0.09375, ((0, 4), (1, 8)))
    router_weight = centred(arg_keys[5], (MODEL_WIDTH, EXPERTS), MODEL_WIDTH ** -0.5, 0.09375)
    expert_in = centred(arg_keys[6], (EXPERTS, MODEL_WIDTH, 2, FF), MODEL_WIDTH ** -0.5, 0.09375, ((0, 4), (3, 8)))
    expert_down = noise_with(arg_keys[7], (EXPERTS, FF, MODEL_WIDTH), FF ** -0.5, 0.09375, ((0, 4), (1, 8)), (1, 2, 8, 2.0))
    kv_cache = draw_kv_cache(jax.random.fold_in(arg_keys[13], 71), 0)
    lengths = draw_lengths(jax.random.fold_in(arg_keys[13], 71), 0)
    tables = draw_tables(jax.random.fold_in(arg_keys[13], 71), 0)
    parents = draw_parents(jax.random.fold_in(arg_keys[13], 71), 0)
    routes_keys = jax.random.split(jax.random.fold_in(arg_keys[12], 1), DECODE_STEPS * BEAM_TOTAL // BEAM_TOTAL)
    routes_turns = jax.random.permutation(jax.random.fold_in(arg_keys[12], 3), DECODE_STEPS * BEAM_TOTAL // BEAM_TOTAL)
    routes = jax.vmap(lambda own, number: assign_block(jax.random.fold_in(arg_keys[12], 2), own, number, BEAM_TOTAL, EXPERTS, 2, CAP, 2))(routes_keys, routes_turns).reshape((DECODE_STEPS, BEAM_TOTAL, 2))
    return dict(hidden_in=hidden_in, attn_gain=attn_gain, ffn_gain=ffn_gain, query_key_value_weight=query_key_value_weight, out_weight=out_weight, router_weight=router_weight, expert_in=expert_in, expert_down=expert_down, kv_cache=kv_cache, lengths=lengths, tables=tables, parents=parents, routes=routes)


NORM_FLOOR = 1e-05
ROPE_BASE = 1000000.0
NEG_FILL = -1e+30

def rotate_pairs(vectors, positions):
    half_width = vectors.shape[-1] // 2
    exponents = jnp.arange(half_width, dtype=jnp.float32) * (2.0 / vectors.shape[-1])
    frequency = ROPE_BASE ** (-exponents)
    angles = positions.astype(jnp.float32)[..., None] * frequency
    cosine = jnp.cos(angles)
    sine_part = jnp.sin(angles)
    lower_half = vectors[..., :half_width]
    upper_half = vectors[..., half_width:]
    return jnp.concatenate([lower_half * cosine - upper_half * sine_part, upper_half * cosine + lower_half * sine_part], axis=-1)

def lineage(parents):
    steps_count, beam_count = parents.shape
    beam_ids = jnp.arange(beam_count, dtype=jnp.int32)
    line_rows = []
    anchor_rows = []
    for step_index in range(steps_count):
        current = beam_ids
        levels = [jnp.full((beam_count,), -1, jnp.int32) for level_index in range(steps_count)]
        for level_index in range(step_index, -1, -1):
            levels[level_index] = current
            current = parents[level_index][current].astype(jnp.int32)
        line_rows.append(jnp.stack(levels))
        anchor_rows.append(current)
    return (jnp.stack(line_rows), jnp.stack(anchor_rows))

def expert_rank(routes):
    steps_count, beam_count, pick_count = routes.shape
    onehot = (routes[..., None] == jnp.arange(EXPERTS, dtype=jnp.int32)).astype(jnp.int32)
    flat_hits = onehot.reshape(steps_count, beam_count * pick_count, EXPERTS)
    before = jnp.cumsum(flat_hits, axis=1) - flat_hits
    return lax.optimization_barrier(jnp.sum(before * flat_hits, axis=-1)).reshape(steps_count, beam_count, pick_count).astype(jnp.int32)

def reference(hidden_in, attn_gain, ffn_gain, query_key_value_weight, out_weight, router_weight, expert_in, expert_down, kv_cache, lengths, tables, parents, routes):
    count_tokens = DECODE_STEPS * BEAM_TOTAL
    logit_scale = 1.0 / math.sqrt(HEAD_WIDTH)
    line_beams, anchor = lineage(parents)
    flat_in = hidden_in.reshape(count_tokens, MODEL_WIDTH).astype(jnp.float32)
    attention_mean = lax.optimization_barrier(jnp.mean(flat_in * flat_in, axis=1))
    pre_attn = (flat_in * attn_gain.astype(jnp.float32)).astype(jnp.bfloat16)
    projected_rows = jnp.dot(pre_attn, query_key_value_weight.reshape(MODEL_WIDTH, -1), preferred_element_type=jnp.float32)
    projected_rows = (projected_rows * lax.rsqrt(attention_mean + NORM_FLOOR)[:, None]).reshape(DECODE_STEPS, BEAM_TOTAL, KEY_VALUE_HEADS, QUERIES_PER_KEY + 2, HEAD_WIDTH)
    beam_groups = jnp.arange(BEAM_TOTAL, dtype=jnp.int32) // BEAM_W
    positions = lengths[beam_groups][None, :] + jnp.arange(DECODE_STEPS, dtype=jnp.int32)[:, None]
    queries = rotate_pairs(projected_rows[:, :, :, :QUERIES_PER_KEY], positions[:, :, None, None]).astype(jnp.bfloat16)
    new_key = rotate_pairs(projected_rows[:, :, :, QUERIES_PER_KEY], positions[:, :, None]).astype(jnp.bfloat16)
    new_value = projected_rows[:, :, :, QUERIES_PER_KEY + 1].astype(jnp.bfloat16)
    recent_allowed = jnp.transpose(line_beams[:, :, :, None] == jnp.arange(BEAM_TOTAL, dtype=jnp.int32), (0, 2, 1, 3)).reshape(DECODE_STEPS, BEAM_TOTAL, count_tokens)
    cache_allowed = jnp.arange(BEAM_BLOCKS * BLOCK_POSITIONS, dtype=jnp.int32)[None, :] < lengths[beam_groups][:, None]
    slot_rows = tables[anchor]

    def attend_heads(combined):
        head_index = combined // DECODE_STEPS
        step_index = combined % DECODE_STEPS
        cache_head = lax.dynamic_index_in_dim(kv_cache, head_index, axis=2, keepdims=False)
        picked = cache_head[lax.dynamic_index_in_dim(slot_rows, step_index, axis=0, keepdims=False)]
        key_matrix = picked[:, :, 0].reshape(BEAM_TOTAL, BEAM_BLOCKS * BLOCK_POSITIONS, HEAD_WIDTH).astype(jnp.float32)
        value_matrix = picked[:, :, 1].reshape(BEAM_TOTAL, BEAM_BLOCKS * BLOCK_POSITIONS, HEAD_WIDTH).astype(jnp.float32)
        query_matrix = lax.dynamic_index_in_dim(queries, step_index, axis=0, keepdims=False)
        query_matrix = lax.dynamic_index_in_dim(query_matrix, head_index, axis=1, keepdims=False).astype(jnp.float32)
        newest_keys = lax.dynamic_index_in_dim(new_key, head_index, axis=2, keepdims=False).reshape(count_tokens, HEAD_WIDTH).astype(jnp.float32)
        newest_values = lax.dynamic_index_in_dim(new_value, head_index, axis=2, keepdims=False).reshape(count_tokens, HEAD_WIDTH).astype(jnp.float32)
        cache_logits = jnp.einsum('uho,ulo->uhl', query_matrix, key_matrix) * logit_scale
        newest_logits = jnp.einsum('scr,xr->scx', query_matrix, newest_keys) * logit_scale
        recent_ok = lax.dynamic_index_in_dim(recent_allowed, step_index, axis=0, keepdims=False)[:, None, :]
        cache_ok = cache_allowed[:, None, :]
        cache_masked = jnp.where(cache_ok, cache_logits, NEG_FILL)
        recent_masked = jnp.where(recent_ok, newest_logits, NEG_FILL)
        row_max = jnp.maximum(lax.optimization_barrier(jnp.max(cache_masked, axis=-1)), lax.optimization_barrier(jnp.max(recent_masked, axis=-1)))[..., None]
        cache_weights = jnp.where(cache_ok, jnp.exp(cache_masked - row_max), 0.0)
        recent_weights = jnp.where(recent_ok, jnp.exp(recent_masked - row_max), 0.0)
        weight_sum = lax.optimization_barrier(jnp.sum(cache_weights, axis=-1)) + lax.optimization_barrier(jnp.sum(recent_weights, axis=-1))
        cache_lowered = lax.optimization_barrier(cache_weights.astype(jnp.bfloat16)).astype(jnp.float32)
        newest_lowered = lax.optimization_barrier(recent_weights.astype(jnp.bfloat16)).astype(jnp.float32)
        weighted_values = jnp.einsum('ufk,uke->ufe', cache_lowered, value_matrix) + jnp.einsum('wrx,xc->wrc', newest_lowered, newest_values)
        return (weighted_values / weight_sum[..., None]).astype(jnp.bfloat16)
    attended_rows = lax.map(attend_heads, jnp.arange(KEY_VALUE_HEADS * DECODE_STEPS, dtype=jnp.int32))
    attended_rows = attended_rows.reshape(KEY_VALUE_HEADS, DECODE_STEPS, BEAM_TOTAL, QUERIES_PER_KEY, HEAD_WIDTH).transpose(1, 2, 0, 3, 4).reshape(count_tokens, QUERY_HEADS * HEAD_WIDTH)
    attn_out = jnp.dot(attended_rows, out_weight, preferred_element_type=jnp.float32)
    residual = (flat_in + attn_out).astype(jnp.bfloat16)
    residual_wide = residual.astype(jnp.float32)
    mean_ffn = lax.optimization_barrier(jnp.mean(residual_wide * residual_wide, axis=1))
    inv_ffn = lax.rsqrt(mean_ffn + NORM_FLOOR)
    pre_ffn = (residual_wide * ffn_gain.astype(jnp.float32)).astype(jnp.bfloat16)
    logits = jnp.dot(pre_ffn, router_weight, preferred_element_type=jnp.float32) * inv_ffn[:, None]
    flat_routes = routes.reshape(count_tokens, 2)
    own_logit = jnp.take_along_axis(logits, flat_routes, axis=1)
    gate_share = 1.0 / (1.0 + jnp.exp(own_logit[:, ::-1] - own_logit))
    rank = expert_rank(routes).reshape(count_tokens, 2)
    rows_per_expert = DECODE_STEPS * CAP
    step_of = jnp.arange(count_tokens, dtype=jnp.int32) // BEAM_TOTAL
    row_id = (flat_routes * rows_per_expert + step_of[:, None] * CAP + rank).reshape(-1)
    token_ids = jnp.broadcast_to(jnp.arange(count_tokens, dtype=jnp.int32)[:, None], (count_tokens, 2)).reshape(-1)
    row_token = jnp.zeros((EXPERTS * rows_per_expert,), jnp.int32).at[row_id].set(token_ids)
    row_gate = jnp.zeros((EXPERTS * rows_per_expert,), jnp.float32).at[row_id].set(gate_share.reshape(-1))

    def run_expert(expert_index):
        rows_here = lax.dynamic_slice_in_dim(row_token, expert_index * rows_per_expert, rows_per_expert)
        pre_rows = pre_ffn[rows_here]
        scale_rows = inv_ffn[rows_here]
        weight_in = lax.dynamic_index_in_dim(expert_in, expert_index, axis=0, keepdims=False).reshape(MODEL_WIDTH, 2 * FF)
        weight_down = lax.dynamic_index_in_dim(expert_down, expert_index, axis=0, keepdims=False)
        expert_act = jnp.dot(pre_rows, weight_in, preferred_element_type=jnp.float32) * scale_rows[:, None]
        expert_hidden = (jax.nn.silu(expert_act[:, :FF]) * expert_act[:, FF:]).astype(jnp.bfloat16)
        return jnp.dot(expert_hidden, weight_down, preferred_element_type=jnp.float32)
    expert_result = lax.map(run_expert, jnp.arange(EXPERTS, dtype=jnp.int32)).reshape(EXPERTS * rows_per_expert, MODEL_WIDTH)
    mixture = jnp.zeros((count_tokens, MODEL_WIDTH), jnp.float32).at[row_token].add(expert_result * row_gate[:, None])
    return (residual_wide + mixture).astype(jnp.bfloat16).reshape(DECODE_STEPS, BEAM_TOTAL, MODEL_WIDTH)
```

```python
import functools
import math

import jax
import jax.numpy as jnp
from jax import lax
from jax.experimental import pallas as pl
from jax.experimental.pallas import tpu as pltpu
from jax.sharding import PartitionSpec as P

MODEL_WIDTH = 4096
HEAD_WIDTH = 128
QUERIES_PER_KEY = 4
EXPERTS = 8
BEAM_W = 8
GROUPS = 2
DECODE_STEPS = 4
BLOCK_POSITIONS = 128
BEAM_BLOCKS = 128
BEAM_TOTAL = 16
CAP = 6


NORM_FLOOR = 1e-05
ROPE_BASE = 1000000.0
NEG_FILL = -1e30


def joined(value, axis, join):
    pieces = jax.tree.map(lambda part: lax.all_gather(part, axis), value)
    head = jax.tree.map(lambda part: part[0], pieces)
    tail = jax.tree.map(lambda part: part[1:], pieces)
    running, _ = lax.scan(lambda running, section: (join(running, section), None), head, tail)
    return running


def rotate_pairs(vectors, positions):
    half_width = vectors.shape[-1] // 2
    exponents = jnp.arange(half_width, dtype=jnp.float32) * (2.0 / vectors.shape[-1])
    frequency = ROPE_BASE ** (-exponents)
    angles = positions.astype(jnp.float32)[..., None] * frequency
    cosine = jnp.cos(angles)
    sine_part = jnp.sin(angles)
    lower_half = vectors[..., :half_width]
    upper_half = vectors[..., half_width:]
    return jnp.concatenate(
        [
            lower_half * cosine - upper_half * sine_part,
            upper_half * cosine + lower_half * sine_part,
        ],
        axis=-1,
    )


def lineage(parents):
    steps_count, beam_count = parents.shape
    beam_ids = jnp.arange(beam_count, dtype=jnp.int32)
    line_rows = []
    anchor_rows = []
    for step_index in range(steps_count):
        current = beam_ids
        levels = [jnp.full((beam_count,), -1, jnp.int32) for level_index in range(steps_count)]
        for level_index in range(step_index, -1, -1):
            levels[level_index] = current
            current = parents[level_index][current]
        line_rows.append(jnp.stack(levels))
        anchor_rows.append(current)
    return (jnp.stack(line_rows), jnp.stack(anchor_rows))


def expert_rank(routes):
    steps_count, beam_count, pick_count = routes.shape
    onehot = (routes[..., None] == jnp.arange(EXPERTS, dtype=jnp.int32)).astype(jnp.int32)
    flat_hits = onehot.reshape(steps_count, beam_count * pick_count, EXPERTS)
    before = jnp.cumsum(flat_hits, axis=1) - flat_hits
    return jnp.sum(before * flat_hits, axis=-1).reshape(steps_count, beam_count, pick_count)


def head_total(partial_value):
    return lax.psum(partial_value, "kv")


def combine_parts(part_one, part_two):
    max_one, sum_one, vector_one = part_one
    max_two, sum_two, vector_two = part_two
    larger = jnp.maximum(max_one, max_two)
    scale_one = jnp.exp(max_one - larger)
    scale_two = jnp.exp(max_two - larger)
    return (
        larger,
        sum_one * scale_one + sum_two * scale_two,
        vector_one * scale_one[..., None] + vector_two * scale_two[..., None],
    )


def groups_to_beams(grouped):
    shaped = grouped.reshape((GROUPS, DECODE_STEPS, BEAM_W, QUERIES_PER_KEY) + grouped.shape[2:])
    shaped = jnp.moveaxis(shaped, 1, 0)
    return shaped.reshape((DECODE_STEPS, BEAM_TOTAL, QUERIES_PER_KEY) + grouped.shape[2:])


def body(
    hidden_in,
    attn_gain,
    ffn_gain,
    query_key_value_weight,
    out_weight,
    router_weight,
    expert_in,
    expert_down,
    kv_cache,
    lengths,
    tables,
    parents,
    routes,
):
    count_tokens = DECODE_STEPS * BEAM_TOTAL
    width_local = hidden_in.shape[2]
    heads_local = query_key_value_weight.shape[1]
    logit_scale = 1.0 / math.sqrt(HEAD_WIDTH)
    line_beams, anchor = lineage(parents)
    flat_in = hidden_in.reshape(count_tokens, width_local).astype(jnp.float32)
    pre_attn = (flat_in * attn_gain.astype(jnp.float32)).astype(jnp.bfloat16)
    partial_proj = jnp.dot(
        pre_attn,
        query_key_value_weight.reshape(width_local, -1),
        preferred_element_type=jnp.float32,
    )
    partial_sq = jnp.sum(flat_in * flat_in, axis=1)
    projected_rows, square_sum = lax.psum((partial_proj, partial_sq), "blk")
    projected_rows = (
        projected_rows * lax.rsqrt(square_sum / MODEL_WIDTH + NORM_FLOOR)[:, None]
    ).reshape(DECODE_STEPS, BEAM_TOTAL, heads_local, QUERIES_PER_KEY + 2, HEAD_WIDTH)
    beam_groups = jnp.arange(BEAM_TOTAL, dtype=jnp.int32) // BEAM_W
    positions = lengths[beam_groups][None, :] + jnp.arange(DECODE_STEPS, dtype=jnp.int32)[:, None]
    queries = rotate_pairs(
        projected_rows[:, :, :, :QUERIES_PER_KEY], positions[:, :, None, None]
    ).astype(jnp.bfloat16)
    new_key = rotate_pairs(projected_rows[:, :, :, QUERIES_PER_KEY], positions[:, :, None]).astype(
        jnp.bfloat16
    )
    new_value = projected_rows[:, :, :, QUERIES_PER_KEY + 1].astype(jnp.bfloat16)
    slot_count = kv_cache.shape[0]
    slot_base = lax.axis_index("blk") * slot_count
    entry_ids = jnp.arange(BEAM_TOTAL * BEAM_BLOCKS, dtype=jnp.int32)
    owner_all = (
        jnp.zeros((BEAM_TOTAL * BEAM_BLOCKS,), jnp.int32)
        .at[tables.reshape(-1)]
        .set(entry_ids // BEAM_BLOCKS)
    )
    block_all = (
        jnp.zeros((BEAM_TOTAL * BEAM_BLOCKS,), jnp.int32)
        .at[tables.reshape(-1)]
        .set(entry_ids % BEAM_BLOCKS)
    )
    owner_here = lax.dynamic_slice_in_dim(owner_all, slot_base, slot_count)
    block_here = lax.dynamic_slice_in_dim(block_all, slot_base, slot_count)
    group_here = owner_here // BEAM_W
    live_keys = (
        block_here[:, None] * BLOCK_POSITIONS
        + jnp.arange(BLOCK_POSITIONS, dtype=jnp.int32)[None, :]
        < lengths[group_here][:, None]
    )
    anchor_groups = jnp.moveaxis(anchor.reshape(DECODE_STEPS, GROUPS, BEAM_W), 1, 0)
    anchor_query = jnp.broadcast_to(
        anchor_groups[..., None], (GROUPS, DECODE_STEPS, BEAM_W, QUERIES_PER_KEY)
    ).reshape(GROUPS, -1)
    query_match = anchor_query[group_here] == owner_here[:, None]
    group_hits = group_here[:, None] == jnp.arange(GROUPS, dtype=jnp.int32)[None, :]
    group_float = group_hits.astype(jnp.float32)
    recent_allowed = jnp.transpose(
        line_beams[:, :, :, None] == jnp.arange(BEAM_TOTAL, dtype=jnp.int32), (0, 2, 1, 3)
    ).reshape(DECODE_STEPS, BEAM_TOTAL, 1, count_tokens)
    is_first = lax.axis_index("blk") == 0
    max_heads = []
    sum_heads = []
    vector_heads = []
    for head_index in range(heads_local):
        query_head = queries[:, :, head_index]
        query_groups = jnp.moveaxis(
            query_head.reshape(DECODE_STEPS, GROUPS, BEAM_W, QUERIES_PER_KEY, HEAD_WIDTH), 1, 0
        ).reshape(GROUPS, -1, HEAD_WIDTH)
        query_slots = query_groups[group_here]
        key_matrix = kv_cache[:, 0, head_index]
        value_matrix = kv_cache[:, 1, head_index]
        scores = (
            jnp.einsum("ptd,pqd->ptq", key_matrix, query_slots, preferred_element_type=jnp.float32)
            * logit_scale
        )
        allowed = live_keys[:, :, None] & query_match[:, None, :]
        masked = jnp.where(allowed, scores, NEG_FILL)
        slot_max = jnp.max(masked, axis=1)
        weights = jnp.where(allowed, jnp.exp(masked - slot_max[:, None, :]), 0.0)
        slot_sum = jnp.sum(weights, axis=1)
        slot_vector = jnp.einsum(
            "ptq,ptd->pqd",
            weights.astype(jnp.bfloat16),
            value_matrix,
            preferred_element_type=jnp.float32,
        )
        group_max = jnp.max(
            jnp.where(group_hits[:, :, None], slot_max[:, None, :], NEG_FILL), axis=0
        )
        rescale = jnp.exp(slot_max - group_max[group_here])
        group_sum = jnp.einsum(
            "pg,pq->gq", group_float, slot_sum * rescale, precision=lax.Precision.HIGHEST
        )
        group_vector = jnp.einsum(
            "pg,pqd->gqd",
            group_float,
            slot_vector * rescale[:, :, None],
            precision=lax.Precision.HIGHEST,
        )
        cache_max = groups_to_beams(group_max)
        cache_sum = groups_to_beams(group_sum)
        cache_vector = groups_to_beams(group_vector)
        newest_keys = new_key[:, :, head_index].reshape(count_tokens, HEAD_WIDTH)
        newest_values = new_value[:, :, head_index].reshape(count_tokens, HEAD_WIDTH)
        newest_logits = (
            jnp.einsum("sbqd,kd->sbqk", query_head, newest_keys, preferred_element_type=jnp.float32)
            * logit_scale
        )
        recent_masked = jnp.where(recent_allowed, newest_logits, NEG_FILL)
        recent_max = jnp.max(recent_masked, axis=-1)
        recent_weights = jnp.where(
            recent_allowed, jnp.exp(recent_masked - recent_max[..., None]), 0.0
        )
        recent_sum = jnp.sum(recent_weights, axis=-1)
        recent_vector = jnp.einsum(
            "sbqk,kd->sbqd",
            recent_weights.astype(jnp.bfloat16),
            newest_values,
            preferred_element_type=jnp.float32,
        )
        recent_max = jnp.where(is_first, recent_max, NEG_FILL)
        recent_sum = jnp.where(is_first, recent_sum, 0.0)
        recent_vector = jnp.where(is_first, recent_vector, 0.0)
        local_max, local_sum, local_vector = combine_parts(
            (cache_max, cache_sum, cache_vector), (recent_max, recent_sum, recent_vector)
        )
        max_heads.append(local_max)
        sum_heads.append(local_sum)
        vector_heads.append(local_vector)
    part_max = jnp.stack(max_heads, axis=2)
    part_sum = jnp.stack(sum_heads, axis=2)
    part_vector = jnp.stack(vector_heads, axis=2)
    whole_max, whole_sum, whole_vector = joined(
        (part_max, part_sum, part_vector), "blk", combine_parts
    )
    attended_rows = (
        (whole_vector / whole_sum[..., None]).astype(jnp.bfloat16).reshape(count_tokens, -1)
    )
    attn_partial = jnp.dot(attended_rows, out_weight, preferred_element_type=jnp.float32)
    attn_out = head_total(attn_partial)
    residual = (flat_in + attn_out).astype(jnp.bfloat16)
    experts_local = expert_in.shape[0]
    ff_local = expert_in.shape[3]
    rows_per_expert = DECODE_STEPS * CAP
    rows_local = experts_local * rows_per_expert
    flat_routes = routes.reshape(count_tokens, 2)
    rank = expert_rank(routes).reshape(count_tokens, 2)
    step_of = jnp.arange(count_tokens, dtype=jnp.int32) // BEAM_TOTAL
    row_id = (flat_routes * rows_per_expert + step_of[:, None] * CAP + rank).reshape(-1)
    token_ids = jnp.broadcast_to(
        jnp.arange(count_tokens, dtype=jnp.int32)[:, None], (count_tokens, 2)
    ).reshape(-1)
    table_size = EXPERTS * rows_per_expert
    row_token_all = jnp.zeros((table_size,), jnp.int32).at[row_id].set(token_ids)
    row_live_all = jnp.zeros((table_size,), jnp.float32).at[row_id].set(1.0)
    row_other_all = (
        jnp.zeros((table_size,), jnp.int32).at[row_id].set(flat_routes[:, ::-1].reshape(-1))
    )
    row_start = lax.axis_index("kv") * rows_local
    row_token = lax.dynamic_slice_in_dim(row_token_all, row_start, rows_local)
    row_live = lax.dynamic_slice_in_dim(row_live_all, row_start, rows_local)
    row_other = lax.dynamic_slice_in_dim(row_other_all, row_start, rows_local)
    row_own = (row_start + jnp.arange(rows_local, dtype=jnp.int32)) // rows_per_expert
    in_flat = expert_in.reshape(experts_local, MODEL_WIDTH, 2 * ff_local)
    gain_wide = ffn_gain.astype(jnp.float32)
    full_rows = lax.all_gather(residual, "blk", axis=1, tiled=True)
    chosen = full_rows[row_token].astype(jnp.float32)
    pre_rows = (chosen * gain_wide).astype(jnp.bfloat16)
    sums_in = jnp.einsum(
        "erd,edf->erf",
        pre_rows.reshape(experts_local, rows_per_expert, MODEL_WIDTH),
        in_flat,
        preferred_element_type=jnp.float32,
    )
    sums_router = jnp.dot(pre_rows, router_weight, preferred_element_type=jnp.float32)
    sum_sq = jnp.sum(chosen * chosen, axis=1)
    inv_rows = lax.rsqrt(sum_sq / MODEL_WIDTH + NORM_FLOOR)
    expert_act = sums_in * inv_rows.reshape(experts_local, rows_per_expert)[:, :, None]
    expert_hidden = (jax.nn.silu(expert_act[..., :ff_local]) * expert_act[..., ff_local:]).astype(
        jnp.bfloat16
    )
    down_part = jnp.einsum(
        "erf,efd->erd", expert_hidden, expert_down, preferred_element_type=jnp.float32
    ).reshape(rows_local, MODEL_WIDTH)
    expert_result = lax.psum_scatter(down_part, "blk", scatter_dimension=1, tiled=True)
    logits = sums_router * inv_rows[:, None]
    expert_ids = jnp.arange(EXPERTS, dtype=jnp.int32)
    own_logit = jnp.sum(jnp.where(row_own[:, None] == expert_ids[None, :], logits, 0.0), axis=1)
    other_logit = jnp.sum(jnp.where(row_other[:, None] == expert_ids[None, :], logits, 0.0), axis=1)
    gate_share = row_live / (1.0 + jnp.exp(other_logit - own_logit))
    weighted_values = expert_result * gate_share[:, None]
    placement = (row_token[None, :] == jnp.arange(count_tokens, dtype=jnp.int32)[:, None]).astype(
        jnp.float32
    )
    mixture_part = jnp.dot(placement, weighted_values, precision=lax.Precision.HIGHEST)
    mixture = head_total(mixture_part)
    layer_out = (residual.astype(jnp.float32) + mixture).astype(jnp.bfloat16)
    return layer_out.reshape(DECODE_STEPS, BEAM_TOTAL, width_local)


MASKED = -3e38
CHUNK = 8
DEPTH = 6
MESH_IDS = pl.DeviceIdType.MESH


def dot32(left, right):
    return jnp.dot(left, right, preferred_element_type=jnp.float32)


def dot32_t(left, right):
    return lax.dot_general(left, right, (((1,), (1,)), ((), ())), preferred_element_type=jnp.float32)


def spread_matrix():
    rows = lax.broadcasted_iota(jnp.int32, (256, 512), 0)
    columns = lax.broadcasted_iota(jnp.int32, (256, 512), 1)
    return jnp.where(columns == 2 * rows, 1.0, 0.0).astype(jnp.bfloat16)


def spread(values, matrix, target, start):
    for piece in range(values.shape[1] // 256):
        even = dot32(values[:, piece * 256 : piece * 256 + 256], matrix)
        odd = pltpu.roll(even, 1, 1)
        first = start + piece * 512
        target[0:64, first : first + 512] = even.astype(jnp.bfloat16)
        target[64:128, first : first + 512] = odd.astype(jnp.bfloat16)


def greet(parts):
    barrier = pltpu.get_barrier_semaphore()
    count = 0
    for axis, size in parts:
        me = lax.axis_index(axis)
        for off in range(1, size):
            pl.semaphore_signal(
                barrier,
                inc=1,
                device_id={axis: lax.rem(me + off, size)},
                device_id_type=MESH_IDS,
            )
            count += 1
    pl.semaphore_wait(barrier, count)


def push(source, target, send, receive, axis, peer):
    copy = pltpu.make_async_remote_copy(
        src_ref=source,
        dst_ref=target,
        send_sem=send,
        recv_sem=receive,
        device_id={axis: peer},
        device_id_type=MESH_IDS,
    )
    copy.start()
    return copy


def project_kernel(
    blk_size, x_ref, gain_ref, w_ref, cos_ref, sin_ref, out_ref, wide, part, got, send1, recv1, send2, recv2
):
    me = lax.axis_index("blk")
    greet((("blk", blk_size),))
    flat = x_ref[...].astype(jnp.float32)
    pre = (flat * gain_ref[...].astype(jnp.float32)).astype(jnp.bfloat16)
    spread(pre, spread_matrix(), wide, 0)
    squares = jnp.broadcast_to(jnp.sum(flat * flat, axis=1, keepdims=True), (64, HEAD_WIDTH))
    squares = jnp.concatenate([squares, squares], axis=0)
    high = squares.astype(jnp.bfloat16)
    part[6] = high
    part[7] = (squares - high.astype(jnp.float32)).astype(jnp.bfloat16)
    lhs = wide[...]
    for c in range(0, 6, 2):
        right = jnp.concatenate(
            [w_ref.at[c].reshape(1024, 128)[...], w_ref.at[c + 1].reshape(1024, 128)[...]], axis=1
        )
        both = dot32(lhs, right).astype(jnp.bfloat16)
        part[c] = both[:, :128]
        part[c + 1] = both[:, 128:]

    def rows_of(index):
        start = lax.rem(index, 2) * 64 + (index // 2) * 16
        return pl.ds(pl.multiple_of(start, 16), 16)

    copies = []
    for off in range(1, blk_size):
        peer = lax.rem(me + off, blk_size)
        copies.append(
            push(part.at[:, rows_of(peer)], got.at[off - 1], send1.at[off - 1], recv1.at[off - 1], "blk", peer)
        )
    total = part[:, rows_of(me)].astype(jnp.float32)
    for off in range(1, blk_size):
        copies[off - 1].wait_recv()
        total = total + got[off - 1].astype(jnp.float32)
    inverse = lax.rsqrt((total[6] + total[7]) * (1.0 / MODEL_WIDTH) + NORM_FLOOR)
    token_rows = pl.ds(pl.multiple_of((me // 2) * 16, 16), 16)
    cosine = cos_ref[token_rows, :]
    sine_part = sin_ref[token_rows, :]
    for c in range(6):
        value = total[c] * inverse
        if c < 5:
            value = value * cosine + pltpu.roll(value, 64, 1) * sine_part
        out_ref[me, c] = value.astype(jnp.bfloat16)
    later = []
    for off in range(1, blk_size):
        peer = lax.rem(me + off, blk_size)
        later.append(
            push(out_ref.at[me], out_ref.at[me], send2.at[off - 1], recv2.at[off - 1], "blk", peer)
        )
    for off in range(1, blk_size):
        later[off - 1].wait_recv()
    for off in range(1, blk_size):
        copies[off - 1].wait_send()
        later[off - 1].wait_send()


def attend_kernel(
    list_ref, count_ref, qkv_ref, anchor_ref, recent_ref, cache, acc_ref, ml_ref, q, m, l, acc, ring, sems
):
    scale = 1.0 / math.sqrt(HEAD_WIDTH)
    first_chunks = (count_ref[0] + CHUNK - 1) // CHUNK
    chunks = first_chunks + (count_ref[1] + CHUNK - 1) // CHUNK

    def place(index):
        group = (index >= first_chunks).astype(jnp.int32)
        return group, group * 256 + (index - group * first_chunks) * CHUNK

    def fetch(index):
        slot = lax.rem(index, DEPTH)
        group, base = place(index)
        for b in range(CHUNK):
            block = list_ref[base + b] & 255
            pltpu.make_async_copy(cache.at[block], ring.at[slot, b], sems.at[slot, b]).start()

    for index in range(DEPTH - 1):

        @pl.when(index < chunks)
        def _():
            fetch(jnp.int32(index))

    for group in range(2):
        for head in range(2):
            gh = group * 2 + head
            rows = []
            for step in range(4):
                for c in range(4):
                    rows.append(
                        qkv_ref[step * 2 + head, c].astype(jnp.float32)[group * 8 : group * 8 + 8]
                    )
            query = jnp.concatenate(rows, axis=0).astype(jnp.bfloat16)
            q[gh] = query
            empty = jnp.zeros((64, HEAD_WIDTH), jnp.bfloat16)
            keys = jnp.concatenate([qkv_ref[step * 2 + head, 4] for step in range(4)] + [empty], axis=0)
            values = jnp.concatenate([qkv_ref[step * 2 + head, 5] for step in range(4)] + [empty], axis=0)
            score = jnp.where(recent_ref[group] > 0, dot32_t(query, keys), MASKED)
            top = jnp.maximum(jnp.max(score, axis=1, keepdims=True), NEG_FILL)
            weight = jnp.exp((score - top) * scale)
            m[gh] = jnp.broadcast_to(top, (128, 128))
            l[gh] = weight
            acc[gh] = dot32(weight.astype(jnp.bfloat16), values)

    lane = lax.broadcasted_iota(jnp.int32, (128, 128), 1)

    def step_body(index, carry):
        @pl.when(index + DEPTH - 1 < chunks)
        def _():
            fetch(index + DEPTH - 1)

        slot = lax.rem(index, DEPTH)
        group, base = place(index)
        for b in range(CHUNK):
            pltpu.make_async_copy(cache.at[0], ring.at[slot, b], sems.at[slot, b]).wait()
        anchors = anchor_ref[group]
        allowed = []
        for b in range(CHUNK):
            entry = list_ref[base + b]
            owner = (entry >> 8) & 31
            limit = entry >> 13
            allowed.append(lane < jnp.where(anchors == owner, limit, 0))
        for head in range(2):
            gh = group * 2 + head
            query = q[gh]
            keys = ring[slot, :, 0, head].reshape(CHUNK * 128, 128)
            scores = dot32_t(query, keys)
            masked = [
                jnp.where(allowed[b], scores[:, b * 128 : b * 128 + 128], MASKED) for b in range(CHUNK)
            ]
            top = functools.reduce(jnp.maximum, masked)
            old = m[gh]
            new = jnp.maximum(old, jnp.max(top, axis=1, keepdims=True))
            decay = jnp.exp((old - new) * scale)
            weights = [jnp.exp((part - new) * scale) for part in masked]
            m[gh] = new
            l[gh] = l[gh] * decay + functools.reduce(jnp.add, weights)
            spread_weights = jnp.concatenate([w.astype(jnp.bfloat16) for w in weights], axis=1)
            values = ring[slot, :, 1, head].reshape(CHUNK * 128, 128)
            acc[gh] = acc[gh] * decay + dot32(spread_weights, values)
        return carry

    lax.fori_loop(0, chunks, step_body, 0)
    for gh in range(4):
        total = jnp.broadcast_to(jnp.sum(l[gh], axis=1, keepdims=True), (128, 128))
        ml_ref[gh, 0:8] = jnp.transpose(m[gh])[0:8] * scale
        ml_ref[gh, 8:16] = jnp.transpose(total)[0:8]
        result = acc[gh].astype(jnp.bfloat16)
        acc_ref[gh * 2] = result[:64]
        acc_ref[gh * 2 + 1] = result[64:]


def layer_kernel(
    blk_size,
    kv_size,
    acc_ref,
    ml_ref,
    x_ref,
    wo_ref,
    gain_ref,
    router_ref,
    routes_ref,
    w_in,
    w_down,
    out_ref,
    inbuf,
    downbuf,
    wide,
    hidden,
    got_acc,
    got_ml,
    coef,
    attended,
    opart,
    got_o,
    resid,
    gathered,
    dpart,
    got_d,
    fpart,
    got_f,
    outs,
    in_sem,
    down_sem,
    s_acc,
    r_acc,
    s_ml,
    r_ml,
    s_att,
    r_att,
    s_o,
    r_o,
    s_res,
    r_res,
    s_all,
    r_all,
    s_d,
    r_d,
    s_f,
    r_f,
    s_out,
    r_out,
):
    me = lax.axis_index("blk")
    my_kv = lax.axis_index("kv")
    width = out_ref.shape[1]

    def in_copy(tile):
        return pltpu.make_async_copy(w_in.at[tile // 8, :, lax.rem(tile, 8)], inbuf.at[tile], in_sem.at[tile])

    def down_copy(piece):
        columns = pl.ds(pl.multiple_of(piece * width, width), width)
        return pltpu.make_async_copy(w_down.at[:, columns], downbuf.at[piece], down_sem.at[piece])

    lax.fori_loop(0, 16, lambda tile, c: (in_copy(tile).start(), c)[1], 0)
    lax.fori_loop(0, blk_size, lambda piece, c: (down_copy(piece).start(), c)[1], 0)
    greet((("blk", blk_size), ("kv", kv_size)))

    waits = []
    pairs = []
    for off in range(1, blk_size):
        peer = lax.rem(me + off, blk_size)
        one = push(acc_ref.at[peer], got_acc.at[off - 1], s_acc.at[off - 1], r_acc.at[off - 1], "blk", peer)
        two = push(ml_ref.at[peer // 2], got_ml.at[off - 1], s_ml.at[off - 1], r_ml.at[off - 1], "blk", peer)
        pairs.append((one, two))
        waits += [one, two]
    stats = [ml_ref[me // 2]]
    for off in range(1, blk_size):
        pairs[off - 1][1].wait_recv()
        stats.append(got_ml[off - 1])
    tops = [stat[0:8] for stat in stats]
    best = functools.reduce(jnp.maximum, tops)
    factors = [jnp.exp(top - best) for top in tops]
    total = functools.reduce(jnp.add, [f * stat[8:16] for f, stat in zip(factors, stats)])
    rows = jnp.concatenate([(f / total)[0:1] for f in factors], axis=0)
    coef[...] = jnp.transpose(jnp.concatenate([rows] * 16, axis=0))
    mine = coef[pl.ds(pl.multiple_of(lax.rem(me, 2) * 64, 64), 64), :]
    joint = mine[:, 0:1] * acc_ref[me].astype(jnp.float32)
    for off in range(1, blk_size):
        pairs[off - 1][0].wait_recv()
        joint = joint + mine[:, off : off + 1] * got_acc[off - 1].astype(jnp.float32)
    attended[me] = joint.astype(jnp.bfloat16)
    copies = []
    for off in range(1, blk_size):
        peer = lax.rem(me + off, blk_size)
        copies.append(
            push(attended.at[me], attended.at[me], s_att.at[off - 1], r_att.at[off - 1], "blk", peer)
        )
    for copy in copies:
        copy.wait_recv()
    waits += copies

    heads = []
    for head in range(2):
        blocks = [
            attended[(group * 2 + head) * 2 + half].astype(jnp.float32)
            for half in range(2)
            for group in range(2)
        ]
        for c in range(4):
            rows = []
            for step in range(4):
                for group in range(2):
                    block = blocks[(step // 2) * 2 + group]
                    start = ((step % 2) * 4 + c) * 8
                    rows.append(block[start : start + 8])
            heads.append(jnp.concatenate(rows, axis=0).astype(jnp.bfloat16))
    opart[...] = dot32(jnp.concatenate(heads, axis=1), wo_ref[...]).astype(jnp.bfloat16)

    def step_rows(index):
        return pl.ds(pl.multiple_of(index * 16, 16), 16)

    copies = []
    for off in range(1, kv_size):
        peer = lax.rem(my_kv + off, kv_size)
        copies.append(
            push(opart.at[step_rows(peer)], got_o.at[off - 1], s_o.at[off - 1], r_o.at[off - 1], "kv", peer)
        )
    sums = x_ref[step_rows(my_kv), :].astype(jnp.float32) + opart[step_rows(my_kv), :].astype(jnp.float32)
    for off in range(1, kv_size):
        copies[off - 1].wait_recv()
        sums = sums + got_o[off - 1].astype(jnp.float32)
    waits += copies
    resid[step_rows(my_kv), :] = sums.astype(jnp.bfloat16)
    copies = []
    for off in range(1, kv_size):
        peer = lax.rem(my_kv + off, kv_size)
        copies.append(
            push(
                resid.at[step_rows(my_kv)], resid.at[step_rows(my_kv)], s_res.at[off - 1], r_res.at[off - 1], "kv", peer
            )
        )
    for copy in copies:
        copy.wait_recv()
    waits += copies

    gathered[me] = resid[...]
    core = lax.rem(me, 2)
    partner = me + 1 - 2 * core
    chips = blk_size // 2
    near = push(gathered.at[me], gathered.at[me], s_all.at[0], r_all.at[0], "blk", partner)
    far = []
    for off in range(1, chips):
        peer = lax.rem(me + 2 * off, blk_size)
        far.append(push(gathered.at[me], gathered.at[me], s_all.at[off], r_all.at[off], "blk", peer))
    relays = []
    for off in range(1, chips):
        far[off - 1].wait_recv()
        origin = lax.rem(me + blk_size - 2 * off, blk_size)
        relays.append(
            push(
                gathered.at[origin],
                gathered.at[origin],
                s_all.at[chips - 1 + off],
                r_all.at[chips - 1 + off],
                "blk",
                partner,
            )
        )
    near.wait_recv()
    for copy in relays:
        copy.wait_recv()
    waits += [near] + far + relays

    matrix = spread_matrix()
    squares = jnp.zeros((64, 1), jnp.float32)
    logits = jnp.zeros((64, EXPERTS), jnp.float32)
    for source in range(blk_size):
        values = gathered[source].astype(jnp.float32)
        squares = squares + jnp.sum(values * values, axis=1, keepdims=True)
        first = source * width
        pre = (values * gain_ref[:, first : first + width].astype(jnp.float32)).astype(jnp.bfloat16)
        logits = logits + dot32_t(pre, router_ref[:, first : first + width])
        spread(pre, matrix, wide, 2 * first)
    inverse = lax.rsqrt(squares * (1.0 / MODEL_WIDTH) + NORM_FLOOR)
    logits = logits * inverse
    lane = lax.broadcasted_iota(jnp.int32, (64, EXPERTS), 1)
    pick_one = routes_ref[:, 0:1]
    pick_two = routes_ref[:, 1:2]
    logit_one = jnp.sum(jnp.where(lane == pick_one, logits, 0.0), axis=1, keepdims=True)
    logit_two = jnp.sum(jnp.where(lane == pick_two, logits, 0.0), axis=1, keepdims=True)
    share_one = 1.0 / (1.0 + jnp.exp(logit_two - logit_one))
    share_two = 1.0 / (1.0 + jnp.exp(logit_one - logit_two))
    named = []
    shares = []
    for local in range(2):
        expert = my_kv * 2 + local
        is_one = pick_one == expert
        is_two = pick_two == expert
        named.append(jnp.where(is_one | is_two, 1, 0))
        shares.append(jnp.where(is_one, share_one, jnp.where(is_two, share_two, 0.0)))

    for local in range(2):

        def expert_body(pair, carry, local=local):
            tile = local * 8 + pair * 2
            in_copy(tile).wait()
            in_copy(tile + 1).wait()
            right = jnp.concatenate(
                [inbuf.at[tile].reshape(8192, 128)[...], inbuf.at[tile + 1].reshape(8192, 128)[...]], axis=1
            )
            both = dot32(wide[...], right)
            gate = both[:64] * inverse
            up = both[64:] * inverse
            act = gate / (1.0 + jnp.exp(-gate)) * up * shares[local]
            act = jnp.where(named[local] > 0, act, 0.0)
            hidden[:, pl.ds(pl.multiple_of(local * 1024 + pair * 256, 256), 256)] = act.astype(jnp.bfloat16)
            return carry

        lax.fori_loop(0, 4, expert_body, 0)

    copies = []
    mixed = None
    for off in range(1, blk_size + 1):
        peer = lax.rem(me + off, blk_size)
        down_copy(peer).wait()
        piece = dot32(hidden[...], downbuf[peer])
        if off < blk_size:
            dpart[off - 1] = piece.astype(jnp.bfloat16)
            copies.append(
                push(dpart.at[off - 1], got_d.at[off - 1], s_d.at[off - 1], r_d.at[off - 1], "blk", peer)
            )
        else:
            mixed = piece
    for off in range(1, blk_size):
        copies[off - 1].wait_recv()
        mixed = mixed + got_d[off - 1].astype(jnp.float32)
    waits += copies
    fpart[...] = mixed.astype(jnp.bfloat16)
    copies = []
    for off in range(1, kv_size):
        peer = lax.rem(my_kv + off, kv_size)
        copies.append(
            push(fpart.at[step_rows(peer)], got_f.at[off - 1], s_f.at[off - 1], r_f.at[off - 1], "kv", peer)
        )
    sums = resid[step_rows(my_kv), :].astype(jnp.float32) + fpart[step_rows(my_kv), :].astype(jnp.float32)
    for off in range(1, kv_size):
        copies[off - 1].wait_recv()
        sums = sums + got_f[off - 1].astype(jnp.float32)
    waits += copies
    outs[step_rows(my_kv), :] = sums.astype(jnp.bfloat16)
    copies = []
    for off in range(1, kv_size):
        peer = lax.rem(my_kv + off, kv_size)
        copies.append(
            push(
                outs.at[step_rows(my_kv)], outs.at[step_rows(my_kv)], s_out.at[off - 1], r_out.at[off - 1], "kv", peer
            )
        )
    for copy in copies:
        copy.wait_recv()
    waits += copies
    out_ref[...] = outs[...]
    for copy in waits:
        copy.wait_send()


def lookup(table, index):
    slots = jnp.arange(table.shape[0], dtype=jnp.int32)
    return jnp.sum(jnp.where(index[..., None] == slots, table, 0), axis=-1)


def kernel_body(
    blk_size,
    kv_size,
    hidden_in,
    attn_gain,
    ffn_gain,
    query_key_value_weight,
    out_weight,
    router_weight,
    expert_in,
    expert_down,
    kv_cache,
    lengths,
    tables,
    parents,
    routes,
):
    bf16, f32 = jnp.bfloat16, jnp.float32
    vmem = pl.BlockSpec(memory_space=pltpu.VMEM)
    smem = pl.BlockSpec(memory_space=pltpu.SMEM)
    hbm = pl.BlockSpec(memory_space=pl.ANY)
    dma = pltpu.SemaphoreType.DMA
    width = hidden_in.shape[2]
    x = hidden_in.reshape(64, width)
    half = HEAD_WIDTH // 2
    frequency = ROPE_BASE ** (-(jnp.arange(half, dtype=f32) * (2.0 / HEAD_WIDTH)))
    token = jnp.arange(64, dtype=jnp.int32)
    position = jnp.where((token % 16) < BEAM_W, lengths[0], lengths[1]) + token // 16
    angle = position.astype(f32)[:, None] * frequency
    cosine, sine_part = jnp.cos(angle), jnp.sin(angle)
    cosine = jnp.concatenate([cosine, cosine], axis=1)
    sine_part = jnp.concatenate([-sine_part, sine_part], axis=1)
    w_qkv = query_key_value_weight.reshape(width, 2, 6, 128).transpose(2, 0, 1, 3)
    qkv = pl.pallas_call(
        functools.partial(project_kernel, blk_size),
        out_shape=jax.ShapeDtypeStruct((blk_size, 6, 16, 128), bf16),
        in_specs=[vmem] * 5,
        out_specs=vmem,
        scratch_shapes=[
            pltpu.VMEM((128, 2 * width), bf16),
            pltpu.VMEM((8, 128, 128), bf16),
            pltpu.VMEM((blk_size - 1, 8, 16, 128), bf16),
        ]
        + [dma((blk_size - 1,))] * 4,
        compiler_params=pltpu.CompilerParams(
            collective_id=0, has_side_effects=True, vmem_limit_bytes=24 * 2**20
        ),
        name="project",
    )(x, attn_gain.reshape(1, width), w_qkv, cosine, sine_part)

    steps = jnp.arange(DECODE_STEPS, dtype=jnp.int32)
    current = jnp.broadcast_to(jnp.arange(BEAM_TOTAL, dtype=jnp.int32), (DECODE_STEPS, BEAM_TOTAL))
    chain = [None] * DECODE_STEPS
    for k in range(DECODE_STEPS - 1, -1, -1):
        chain[k] = jnp.where(steps[:, None] >= k, current, -1)
        current = jnp.where(steps[:, None] >= k, lookup(parents[k], current), current)
    anchor = current
    chain = jnp.stack(chain, axis=1)
    by_group = jnp.moveaxis(anchor.reshape(DECODE_STEPS, 2, BEAM_W), 1, 0)
    anchor_rows = jnp.broadcast_to(by_group[:, :, None, :, None], (2, 4, 4, BEAM_W, 128)).reshape(2, 128, 128)
    seen = chain[:, :, :, None] == jnp.arange(BEAM_TOTAL, dtype=jnp.int32)
    seen = jnp.transpose(seen, (0, 2, 1, 3)).reshape(DECODE_STEPS, 2, BEAM_W, 64)
    seen = (seen & (lax.axis_index("blk") == 0)).astype(jnp.int32)
    seen = jnp.pad(jnp.moveaxis(seen, 1, 0), ((0, 0), (0, 0), (0, 0), (0, 64)))
    recent = jnp.broadcast_to(seen[:, :, None], (2, 4, 4, BEAM_W, 128)).reshape(2, 128, 128)

    slot_count = kv_cache.shape[0]
    slots = jnp.arange(slot_count, dtype=jnp.int32)
    flat = tables.reshape(-1)
    entries = jnp.arange(flat.shape[0], dtype=jnp.int32)
    here = (slots + lax.axis_index("blk") * slot_count)[:, None] == flat[None, :]
    entry = jnp.sum(jnp.where(here, entries[None, :], 0), axis=1)
    owner = entry // BEAM_BLOCKS
    start = (entry % BEAM_BLOCKS) * BLOCK_POSITIONS
    group = owner // BEAM_W
    limit = jnp.clip(jnp.where(group == 0, lengths[0], lengths[1]) - start, 0, BLOCK_POSITIONS)
    used = jnp.any(owner[:, None] == anchor.reshape(1, -1), axis=1)
    live = (limit > 0) & used
    packed = slots + owner * 256 + limit * 8192
    member = live[None, :] & (group[None, :] == jnp.arange(2, dtype=jnp.int32)[:, None])
    before = jnp.sum(member[:, None, :] & (slots[None, :] < slots[:, None])[None], axis=2, dtype=jnp.int32)
    chosen = member[:, None, :] & (before[:, None, :] == slots[None, :, None])
    listing = jnp.sum(jnp.where(chosen, packed[None, None, :], 0), axis=2).reshape(-1)
    counts = jnp.sum(member, axis=1, dtype=jnp.int32)

    acc, stats = pl.pallas_call(
        attend_kernel,
        out_shape=(jax.ShapeDtypeStruct((8, 64, 128), bf16), jax.ShapeDtypeStruct((4, 16, 128), f32)),
        in_specs=[smem, smem, vmem, vmem, vmem, hbm],
        out_specs=(vmem, vmem),
        scratch_shapes=[
            pltpu.VMEM((4, 128, 128), bf16),
            pltpu.VMEM((4, 128, 128), f32),
            pltpu.VMEM((4, 128, 128), f32),
            pltpu.VMEM((4, 128, 128), f32),
            pltpu.VMEM((DEPTH, CHUNK, 2, 2, 128, 128), bf16),
            dma((DEPTH, CHUNK)),
        ],
        compiler_params=pltpu.CompilerParams(vmem_limit_bytes=32 * 2**20),
        name="attend",
    )(listing, counts, qkv, anchor_rows, recent, kv_cache)

    w_in = expert_in.reshape(2, MODEL_WIDTH, 2, 8, 128).transpose(0, 1, 3, 2, 4)
    b, k = blk_size - 1, kv_size - 1
    out = pl.pallas_call(
        functools.partial(layer_kernel, blk_size, kv_size),
        out_shape=jax.ShapeDtypeStruct((64, width), bf16),
        in_specs=[vmem] * 7 + [hbm] * 2,
        out_specs=vmem,
        scratch_shapes=[
            pltpu.VMEM((16, MODEL_WIDTH, 2, 128), bf16),
            pltpu.VMEM((blk_size, 2048, width), bf16),
            pltpu.VMEM((128, 2 * MODEL_WIDTH), bf16),
            pltpu.VMEM((64, 2048), bf16),
            pltpu.VMEM((b, 64, 128), bf16),
            pltpu.VMEM((b, 16, 128), f32),
            pltpu.VMEM((128, 128), f32),
            pltpu.VMEM((blk_size, 64, 128), bf16),
            pltpu.VMEM((64, width), bf16),
            pltpu.VMEM((k, 16, width), bf16),
            pltpu.VMEM((64, width), bf16),
            pltpu.VMEM((blk_size, 64, width), bf16),
            pltpu.VMEM((b, 64, width), bf16),
            pltpu.VMEM((b, 64, width), bf16),
            pltpu.VMEM((64, width), bf16),
            pltpu.VMEM((k, 16, width), bf16),
            pltpu.VMEM((64, width), bf16),
            dma((16,)),
            dma((blk_size,)),
        ]
        + [dma((b,))] * 6
        + [dma((k,))] * 4
        + [dma((b,))] * 4
        + [dma((k,))] * 4,
        compiler_params=pltpu.CompilerParams(
            collective_id=1, has_side_effects=True, vmem_limit_bytes=60 * 2**20
        ),
        name="layer",
    )(
        acc,
        stats,
        x,
        out_weight,
        ffn_gain.reshape(1, MODEL_WIDTH),
        router_weight.T,
        routes.reshape(64, 2),
        w_in,
        expert_down.reshape(2048, MODEL_WIDTH),
    )
    return out.reshape(DECODE_STEPS, BEAM_TOTAL, width)


def solution(mesh):
    blk_size, kv_size = mesh.shape["blk"], mesh.shape["kv"]
    if (blk_size, kv_size) == (8, 4):
        run = functools.partial(kernel_body, blk_size, kv_size)
    else:
        run = body
    placed = (
        P(None, None, "blk"),
        P("blk"),
        P(),
        P("blk", "kv", None),
        P("kv", "blk"),
        P(),
        P("kv", None, None, "blk"),
        P("kv", "blk", None),
        P("blk", None, "kv", None, None),
        P(),
        P(),
        P(),
        P(),
    )
    return jax.shard_map(
        run, mesh=mesh, in_specs=placed, out_specs=P(None, None, "blk"), check_vma=False
    )
```

```python
import functools
import math

import jax
import jax.numpy as jnp
from jax import lax
from jax.experimental import pallas as pl
from jax.experimental.pallas import tpu as pltpu
from jax.sharding import PartitionSpec as P

MODEL_WIDTH = 4096
HEAD_WIDTH = 128
QUERIES_PER_KEY = 4
EXPERTS = 8
BEAM_W = 8
GROUPS = 2
DECODE_STEPS = 4
BLOCK_POSITIONS = 128
BEAM_BLOCKS = 128
BEAM_TOTAL = 16
CAP = 6


NORM_FLOOR = 1e-05
ROPE_BASE = 1000000.0
NEG_FILL = -1e30


def joined(value, axis, join):
    pieces = jax.tree.map(lambda part: lax.all_gather(part, axis), value)
    head = jax.tree.map(lambda part: part[0], pieces)
    tail = jax.tree.map(lambda part: part[1:], pieces)
    running, _ = lax.scan(lambda running, section: (join(running, section), None), head, tail)
    return running


def rotate_pairs(vectors, positions):
    half_width = vectors.shape[-1] // 2
    exponents = jnp.arange(half_width, dtype=jnp.float32) * (2.0 / vectors.shape[-1])
    frequency = ROPE_BASE ** (-exponents)
    angles = positions.astype(jnp.float32)[..., None] * frequency
    cosine = jnp.cos(angles)
    sine_part = jnp.sin(angles)
    lower_half = vectors[..., :half_width]
    upper_half = vectors[..., half_width:]
    return jnp.concatenate(
        [
            lower_half * cosine - upper_half * sine_part,
            upper_half * cosine + lower_half * sine_part,
        ],
        axis=-1,
    )


def lineage(parents):
    steps_count, beam_count = parents.shape
    beam_ids = jnp.arange(beam_count, dtype=jnp.int32)
    line_rows = []
    anchor_rows = []
    for step_index in range(steps_count):
        current = beam_ids
        levels = [jnp.full((beam_count,), -1, jnp.int32) for level_index in range(steps_count)]
        for level_index in range(step_index, -1, -1):
            levels[level_index] = current
            current = parents[level_index][current]
        line_rows.append(jnp.stack(levels))
        anchor_rows.append(current)
    return (jnp.stack(line_rows), jnp.stack(anchor_rows))


def expert_rank(routes):
    steps_count, beam_count, pick_count = routes.shape
    onehot = (routes[..., None] == jnp.arange(EXPERTS, dtype=jnp.int32)).astype(jnp.int32)
    flat_hits = onehot.reshape(steps_count, beam_count * pick_count, EXPERTS)
    before = jnp.cumsum(flat_hits, axis=1) - flat_hits
    return jnp.sum(before * flat_hits, axis=-1).reshape(steps_count, beam_count, pick_count)


def head_total(partial_value):
    return lax.psum(partial_value, "kv")


def combine_parts(part_one, part_two):
    max_one, sum_one, vector_one = part_one
    max_two, sum_two, vector_two = part_two
    larger = jnp.maximum(max_one, max_two)
    scale_one = jnp.exp(max_one - larger)
    scale_two = jnp.exp(max_two - larger)
    return (
        larger,
        sum_one * scale_one + sum_two * scale_two,
        vector_one * scale_one[..., None] + vector_two * scale_two[..., None],
    )


def groups_to_beams(grouped):
    shaped = grouped.reshape((GROUPS, DECODE_STEPS, BEAM_W, QUERIES_PER_KEY) + grouped.shape[2:])
    shaped = jnp.moveaxis(shaped, 1, 0)
    return shaped.reshape((DECODE_STEPS, BEAM_TOTAL, QUERIES_PER_KEY) + grouped.shape[2:])


def body(
    hidden_in,
    attn_gain,
    ffn_gain,
    query_key_value_weight,
    out_weight,
    router_weight,
    expert_in,
    expert_down,
    kv_cache,
    lengths,
    tables,
    parents,
    routes,
):
    count_tokens = DECODE_STEPS * BEAM_TOTAL
    width_local = hidden_in.shape[2]
    heads_local = query_key_value_weight.shape[1]
    logit_scale = 1.0 / math.sqrt(HEAD_WIDTH)
    line_beams, anchor = lineage(parents)
    flat_in = hidden_in.reshape(count_tokens, width_local).astype(jnp.float32)
    pre_attn = (flat_in * attn_gain.astype(jnp.float32)).astype(jnp.bfloat16)
    partial_proj = jnp.dot(
        pre_attn,
        query_key_value_weight.reshape(width_local, -1),
        preferred_element_type=jnp.float32,
    )
    partial_sq = jnp.sum(flat_in * flat_in, axis=1)
    projected_rows, square_sum = lax.psum((partial_proj, partial_sq), "blk")
    projected_rows = (
        projected_rows * lax.rsqrt(square_sum / MODEL_WIDTH + NORM_FLOOR)[:, None]
    ).reshape(DECODE_STEPS, BEAM_TOTAL, heads_local, QUERIES_PER_KEY + 2, HEAD_WIDTH)
    beam_groups = jnp.arange(BEAM_TOTAL, dtype=jnp.int32) // BEAM_W
    positions = lengths[beam_groups][None, :] + jnp.arange(DECODE_STEPS, dtype=jnp.int32)[:, None]
    queries = rotate_pairs(
        projected_rows[:, :, :, :QUERIES_PER_KEY], positions[:, :, None, None]
    ).astype(jnp.bfloat16)
    new_key = rotate_pairs(projected_rows[:, :, :, QUERIES_PER_KEY], positions[:, :, None]).astype(
        jnp.bfloat16
    )
    new_value = projected_rows[:, :, :, QUERIES_PER_KEY + 1].astype(jnp.bfloat16)
    slot_count = kv_cache.shape[0]
    slot_base = lax.axis_index("blk") * slot_count
    entry_ids = jnp.arange(BEAM_TOTAL * BEAM_BLOCKS, dtype=jnp.int32)
    owner_all = (
        jnp.zeros((BEAM_TOTAL * BEAM_BLOCKS,), jnp.int32)
        .at[tables.reshape(-1)]
        .set(entry_ids // BEAM_BLOCKS)
    )
    block_all = (
        jnp.zeros((BEAM_TOTAL * BEAM_BLOCKS,), jnp.int32)
        .at[tables.reshape(-1)]
        .set(entry_ids % BEAM_BLOCKS)
    )
    owner_here = lax.dynamic_slice_in_dim(owner_all, slot_base, slot_count)
    block_here = lax.dynamic_slice_in_dim(block_all, slot_base, slot_count)
    group_here = owner_here // BEAM_W
    live_keys = (
        block_here[:, None] * BLOCK_POSITIONS
        + jnp.arange(BLOCK_POSITIONS, dtype=jnp.int32)[None, :]
        < lengths[group_here][:, None]
    )
    anchor_groups = jnp.moveaxis(anchor.reshape(DECODE_STEPS, GROUPS, BEAM_W), 1, 0)
    anchor_query = jnp.broadcast_to(
        anchor_groups[..., None], (GROUPS, DECODE_STEPS, BEAM_W, QUERIES_PER_KEY)
    ).reshape(GROUPS, -1)
    query_match = anchor_query[group_here] == owner_here[:, None]
    group_hits = group_here[:, None] == jnp.arange(GROUPS, dtype=jnp.int32)[None, :]
    group_float = group_hits.astype(jnp.float32)
    recent_allowed = jnp.transpose(
        line_beams[:, :, :, None] == jnp.arange(BEAM_TOTAL, dtype=jnp.int32), (0, 2, 1, 3)
    ).reshape(DECODE_STEPS, BEAM_TOTAL, 1, count_tokens)
    is_first = lax.axis_index("blk") == 0
    max_heads = []
    sum_heads = []
    vector_heads = []
    for head_index in range(heads_local):
        query_head = queries[:, :, head_index]
        query_groups = jnp.moveaxis(
            query_head.reshape(DECODE_STEPS, GROUPS, BEAM_W, QUERIES_PER_KEY, HEAD_WIDTH), 1, 0
        ).reshape(GROUPS, -1, HEAD_WIDTH)
        query_slots = query_groups[group_here]
        key_matrix = kv_cache[:, 0, head_index]
        value_matrix = kv_cache[:, 1, head_index]
        scores = (
            jnp.einsum("ptd,pqd->ptq", key_matrix, query_slots, preferred_element_type=jnp.float32)
            * logit_scale
        )
        allowed = live_keys[:, :, None] & query_match[:, None, :]
        masked = jnp.where(allowed, scores, NEG_FILL)
        slot_max = jnp.max(masked, axis=1)
        weights = jnp.where(allowed, jnp.exp(masked - slot_max[:, None, :]), 0.0)
        slot_sum = jnp.sum(weights, axis=1)
        slot_vector = jnp.einsum(
            "ptq,ptd->pqd",
            weights.astype(jnp.bfloat16),
            value_matrix,
            preferred_element_type=jnp.float32,
        )
        group_max = jnp.max(
            jnp.where(group_hits[:, :, None], slot_max[:, None, :], NEG_FILL), axis=0
        )
        rescale = jnp.exp(slot_max - group_max[group_here])
        group_sum = jnp.einsum(
            "pg,pq->gq", group_float, slot_sum * rescale, precision=lax.Precision.HIGHEST
        )
        group_vector = jnp.einsum(
            "pg,pqd->gqd",
            group_float,
            slot_vector * rescale[:, :, None],
            precision=lax.Precision.HIGHEST,
        )
        cache_max = groups_to_beams(group_max)
        cache_sum = groups_to_beams(group_sum)
        cache_vector = groups_to_beams(group_vector)
        newest_keys = new_key[:, :, head_index].reshape(count_tokens, HEAD_WIDTH)
        newest_values = new_value[:, :, head_index].reshape(count_tokens, HEAD_WIDTH)
        newest_logits = (
            jnp.einsum("sbqd,kd->sbqk", query_head, newest_keys, preferred_element_type=jnp.float32)
            * logit_scale
        )
        recent_masked = jnp.where(recent_allowed, newest_logits, NEG_FILL)
        recent_max = jnp.max(recent_masked, axis=-1)
        recent_weights = jnp.where(
            recent_allowed, jnp.exp(recent_masked - recent_max[..., None]), 0.0
        )
        recent_sum = jnp.sum(recent_weights, axis=-1)
        recent_vector = jnp.einsum(
            "sbqk,kd->sbqd",
            recent_weights.astype(jnp.bfloat16),
            newest_values,
            preferred_element_type=jnp.float32,
        )
        recent_max = jnp.where(is_first, recent_max, NEG_FILL)
        recent_sum = jnp.where(is_first, recent_sum, 0.0)
        recent_vector = jnp.where(is_first, recent_vector, 0.0)
        local_max, local_sum, local_vector = combine_parts(
            (cache_max, cache_sum, cache_vector), (recent_max, recent_sum, recent_vector)
        )
        max_heads.append(local_max)
        sum_heads.append(local_sum)
        vector_heads.append(local_vector)
    part_max = jnp.stack(max_heads, axis=2)
    part_sum = jnp.stack(sum_heads, axis=2)
    part_vector = jnp.stack(vector_heads, axis=2)
    whole_max, whole_sum, whole_vector = joined(
        (part_max, part_sum, part_vector), "blk", combine_parts
    )
    attended_rows = (
        (whole_vector / whole_sum[..., None]).astype(jnp.bfloat16).reshape(count_tokens, -1)
    )
    attn_partial = jnp.dot(attended_rows, out_weight, preferred_element_type=jnp.float32)
    attn_out = head_total(attn_partial)
    residual = (flat_in + attn_out).astype(jnp.bfloat16)
    experts_local = expert_in.shape[0]
    ff_local = expert_in.shape[3]
    rows_per_expert = DECODE_STEPS * CAP
    rows_local = experts_local * rows_per_expert
    flat_routes = routes.reshape(count_tokens, 2)
    rank = expert_rank(routes).reshape(count_tokens, 2)
    step_of = jnp.arange(count_tokens, dtype=jnp.int32) // BEAM_TOTAL
    row_id = (flat_routes * rows_per_expert + step_of[:, None] * CAP + rank).reshape(-1)
    token_ids = jnp.broadcast_to(
        jnp.arange(count_tokens, dtype=jnp.int32)[:, None], (count_tokens, 2)
    ).reshape(-1)
    table_size = EXPERTS * rows_per_expert
    row_token_all = jnp.zeros((table_size,), jnp.int32).at[row_id].set(token_ids)
    row_live_all = jnp.zeros((table_size,), jnp.float32).at[row_id].set(1.0)
    row_other_all = (
        jnp.zeros((table_size,), jnp.int32).at[row_id].set(flat_routes[:, ::-1].reshape(-1))
    )
    row_start = lax.axis_index("kv") * rows_local
    row_token = lax.dynamic_slice_in_dim(row_token_all, row_start, rows_local)
    row_live = lax.dynamic_slice_in_dim(row_live_all, row_start, rows_local)
    row_other = lax.dynamic_slice_in_dim(row_other_all, row_start, rows_local)
    row_own = (row_start + jnp.arange(rows_local, dtype=jnp.int32)) // rows_per_expert
    in_flat = expert_in.reshape(experts_local, MODEL_WIDTH, 2 * ff_local)
    gain_wide = ffn_gain.astype(jnp.float32)
    full_rows = lax.all_gather(residual, "blk", axis=1, tiled=True)
    chosen = full_rows[row_token].astype(jnp.float32)
    pre_rows = (chosen * gain_wide).astype(jnp.bfloat16)
    sums_in = jnp.einsum(
        "erd,edf->erf",
        pre_rows.reshape(experts_local, rows_per_expert, MODEL_WIDTH),
        in_flat,
        preferred_element_type=jnp.float32,
    )
    sums_router = jnp.dot(pre_rows, router_weight, preferred_element_type=jnp.float32)
    sum_sq = jnp.sum(chosen * chosen, axis=1)
    inv_rows = lax.rsqrt(sum_sq / MODEL_WIDTH + NORM_FLOOR)
    expert_act = sums_in * inv_rows.reshape(experts_local, rows_per_expert)[:, :, None]
    expert_hidden = (jax.nn.silu(expert_act[..., :ff_local]) * expert_act[..., ff_local:]).astype(
        jnp.bfloat16
    )
    down_part = jnp.einsum(
        "erf,efd->erd", expert_hidden, expert_down, preferred_element_type=jnp.float32
    ).reshape(rows_local, MODEL_WIDTH)
    expert_result = lax.psum_scatter(down_part, "blk", scatter_dimension=1, tiled=True)
    logits = sums_router * inv_rows[:, None]
    expert_ids = jnp.arange(EXPERTS, dtype=jnp.int32)
    own_logit = jnp.sum(jnp.where(row_own[:, None] == expert_ids[None, :], logits, 0.0), axis=1)
    other_logit = jnp.sum(jnp.where(row_other[:, None] == expert_ids[None, :], logits, 0.0), axis=1)
    gate_share = row_live / (1.0 + jnp.exp(other_logit - own_logit))
    weighted_values = expert_result * gate_share[:, None]
    placement = (row_token[None, :] == jnp.arange(count_tokens, dtype=jnp.int32)[:, None]).astype(
        jnp.float32
    )
    mixture_part = jnp.dot(placement, weighted_values, precision=lax.Precision.HIGHEST)
    mixture = head_total(mixture_part)
    layer_out = (residual.astype(jnp.float32) + mixture).astype(jnp.bfloat16)
    return layer_out.reshape(DECODE_STEPS, BEAM_TOTAL, width_local)


MASKED = -3e38
CHUNK = 8
DEPTH = 6
MESH_IDS = pl.DeviceIdType.MESH


def dot32(left, right):
    return jnp.dot(left, right, preferred_element_type=jnp.float32)


def dot32_t(left, right):
    return lax.dot_general(left, right, (((1,), (1,)), ((), ())), preferred_element_type=jnp.float32)


def spread_matrix():
    rows = lax.broadcasted_iota(jnp.int32, (256, 512), 0)
    columns = lax.broadcasted_iota(jnp.int32, (256, 512), 1)
    return jnp.where(columns == 2 * rows, 1.0, 0.0).astype(jnp.bfloat16)


def spread(values, matrix, target, start):
    for piece in range(values.shape[1] // 256):
        even = dot32(values[:, piece * 256 : piece * 256 + 256], matrix)
        odd = pltpu.roll(even, 1, 1)
        first = start + piece * 512
        target[0:64, first : first + 512] = even.astype(jnp.bfloat16)
        target[64:128, first : first + 512] = odd.astype(jnp.bfloat16)


def greet(parts):
    barrier = pltpu.get_barrier_semaphore()
    count = 0
    for axis, size in parts:
        me = lax.axis_index(axis)
        for off in range(1, size):
            pl.semaphore_signal(
                barrier,
                inc=1,
                device_id={axis: lax.rem(me + off, size)},
                device_id_type=MESH_IDS,
            )
            count += 1
    pl.semaphore_wait(barrier, count)


def push(source, target, send, receive, axis, peer):
    copy = pltpu.make_async_remote_copy(
        src_ref=source,
        dst_ref=target,
        send_sem=send,
        recv_sem=receive,
        device_id={axis: peer},
        device_id_type=MESH_IDS,
    )
    copy.start()
    return copy


def project_kernel(
    blk_size, x_ref, gain_ref, cos_ref, sin_ref, w_hbm, out_ref, w_ref, wide, part, got, w_sem, send1, recv1, send2, recv2
):
    me = lax.axis_index("blk")
    loads = [pltpu.make_async_copy(w_hbm.at[:, c], w_ref.at[c], w_sem.at[c]) for c in range(6)]
    for load in loads:
        load.start()
    greet((("blk", blk_size),))
    flat = x_ref[...].astype(jnp.float32)
    pre = (flat * gain_ref[...].astype(jnp.float32)).astype(jnp.bfloat16)
    spread(pre, spread_matrix(), wide, 0)
    squares = jnp.broadcast_to(jnp.sum(flat * flat, axis=1, keepdims=True), (64, HEAD_WIDTH))
    squares = jnp.concatenate([squares, squares], axis=0)
    high = squares.astype(jnp.bfloat16)
    part[6] = high
    part[7] = (squares - high.astype(jnp.float32)).astype(jnp.bfloat16)
    lhs = wide[...]
    for c in range(0, 6, 2):
        loads[c].wait()
        loads[c + 1].wait()
        right = jnp.concatenate(
            [w_ref.at[c].reshape(1024, 128)[...], w_ref.at[c + 1].reshape(1024, 128)[...]], axis=1
        )
        both = dot32(lhs, right).astype(jnp.bfloat16)
        part[c] = both[:, :128]
        part[c + 1] = both[:, 128:]

    def rows_of(index):
        start = lax.rem(index, 2) * 64 + (index // 2) * 16
        return pl.ds(pl.multiple_of(start, 16), 16)

    copies = []
    for off in range(1, blk_size):
        peer = lax.rem(me + off, blk_size)
        copies.append(
            push(part.at[:, rows_of(peer)], got.at[off - 1], send1.at[off - 1], recv1.at[off - 1], "blk", peer)
        )
    total = part[:, rows_of(me)].astype(jnp.float32)
    for off in range(1, blk_size):
        copies[off - 1].wait_recv()
        total = total + got[off - 1].astype(jnp.float32)
    inverse = lax.rsqrt((total[6] + total[7]) * (1.0 / MODEL_WIDTH) + NORM_FLOOR)
    token_rows = pl.ds(pl.multiple_of((me // 2) * 16, 16), 16)
    cosine = cos_ref[token_rows, :]
    sine_part = sin_ref[token_rows, :]
    for c in range(6):
        value = total[c] * inverse
        if c < 5:
            value = value * cosine + pltpu.roll(value, 64, 1) * sine_part
        out_ref[me, c] = value.astype(jnp.bfloat16)
    later = []
    for off in range(1, blk_size):
        peer = lax.rem(me + off, blk_size)
        later.append(
            push(out_ref.at[me], out_ref.at[me], send2.at[off - 1], recv2.at[off - 1], "blk", peer)
        )
    for off in range(1, blk_size):
        later[off - 1].wait_recv()
    for off in range(1, blk_size):
        copies[off - 1].wait_send()
        later[off - 1].wait_send()


def attend_kernel(
    list_ref, count_ref, qkv_ref, anchor_ref, recent_ref, cache, acc_ref, ml_ref, q, m, l, acc, ring, sems
):
    scale = 1.0 / math.sqrt(HEAD_WIDTH)
    scale2 = scale * math.log2(math.e)
    first_chunks = (count_ref[0] + CHUNK - 1) // CHUNK
    chunks = first_chunks + (count_ref[1] + CHUNK - 1) // CHUNK

    def place(index):
        group = (index >= first_chunks).astype(jnp.int32)
        return group, group * 256 + (index - group * first_chunks) * CHUNK

    def fetch(index):
        slot = lax.rem(index, DEPTH)
        group, base = place(index)
        for b in range(CHUNK):
            block = list_ref[base + b] & 255
            pltpu.make_async_copy(cache.at[block], ring.at[slot, b], sems.at[slot, b]).start()

    for index in range(DEPTH - 1):

        @pl.when(index < chunks)
        def _():
            fetch(jnp.int32(index))

    for group in range(2):
        for head in range(2):
            gh = group * 2 + head
            rows = []
            for step in range(4):
                for c in range(4):
                    rows.append(
                        qkv_ref[step * 2 + head, c].astype(jnp.float32)[group * 8 : group * 8 + 8]
                    )
            query = jnp.concatenate(rows, axis=0).astype(jnp.bfloat16)
            q[gh] = query
            empty = jnp.zeros((64, HEAD_WIDTH), jnp.bfloat16)
            keys = jnp.concatenate([qkv_ref[step * 2 + head, 4] for step in range(4)] + [empty], axis=0)
            values = jnp.concatenate([qkv_ref[step * 2 + head, 5] for step in range(4)] + [empty], axis=0)
            score = jnp.where(recent_ref[group] > 0, dot32_t(query, keys), MASKED)
            top = jnp.maximum(jnp.max(score, axis=1, keepdims=True), NEG_FILL)
            weight = jnp.exp((score - top) * scale)
            m[gh] = jnp.broadcast_to(top, (128, 128))
            l[gh] = weight
            acc[gh] = dot32(weight.astype(jnp.bfloat16), values)

    lane = lax.broadcasted_iota(jnp.int32, (128, 128), 1)

    def step_body(index, carry):
        @pl.when(index + DEPTH - 1 < chunks)
        def _():
            fetch(index + DEPTH - 1)

        slot = lax.rem(index, DEPTH)
        group, base = place(index)
        for b in range(CHUNK):
            pltpu.make_async_copy(cache.at[0], ring.at[slot, b], sems.at[slot, b]).wait()
        anchors = anchor_ref[group]
        allowed = []
        for b in range(CHUNK):
            entry = list_ref[base + b]
            owner = (entry >> 8) & 31
            limit = entry >> 13
            allowed.append(lane < jnp.where(anchors == owner, limit, 0))
        held = [(m[group * 2 + h], l[group * 2 + h], acc[group * 2 + h]) for h in range(2)]
        scores = [
            dot32_t(q[group * 2 + h], ring[slot, :, 0, h].reshape(CHUNK * 128, 128)) for h in range(2)
        ]
        fresh = []
        for head in range(2):
            old, old_sum, old_acc = held[head]
            masked = [
                jnp.where(allowed[b], scores[head][:, b * 128 : b * 128 + 128], MASKED)
                for b in range(CHUNK)
            ]
            top = functools.reduce(jnp.maximum, masked)
            new = jnp.maximum(old, jnp.max(top, axis=1, keepdims=True))
            decay = jnp.exp2((old - new) * scale2)
            weights = [jnp.exp2((part - new) * scale2) for part in masked]
            new_sum = old_sum * decay + functools.reduce(jnp.add, weights)
            spread_weights = jnp.concatenate([w.astype(jnp.bfloat16) for w in weights], axis=1)
            values = ring[slot, :, 1, head].reshape(CHUNK * 128, 128)
            fresh.append((new, new_sum, old_acc * decay + dot32(spread_weights, values)))
        for head in range(2):
            m[group * 2 + head] = fresh[head][0]
            l[group * 2 + head] = fresh[head][1]
            acc[group * 2 + head] = fresh[head][2]
        return carry

    lax.fori_loop(0, chunks, step_body, 0)
    for gh in range(4):
        total = jnp.broadcast_to(jnp.sum(l[gh], axis=1, keepdims=True), (128, 128))
        ml_ref[gh, 0:8] = jnp.transpose(m[gh])[0:8] * scale
        ml_ref[gh, 8:16] = jnp.transpose(total)[0:8]
        result = acc[gh].astype(jnp.bfloat16)
        acc_ref[gh * 2] = result[:64]
        acc_ref[gh * 2 + 1] = result[64:]


def layer_kernel(
    blk_size,
    kv_size,
    acc_ref,
    ml_ref,
    x_ref,
    wo_ref,
    gain_ref,
    router_ref,
    routes_ref,
    w_in,
    w_down,
    out_ref,
    inbuf,
    downbuf,
    wide,
    hidden,
    got_acc,
    got_ml,
    coef,
    attended,
    opart,
    got_o,
    resid,
    gathered,
    dpart,
    got_d,
    fpart,
    got_f,
    outs,
    sums_in,
    stat_rows,
    logit_rows,
    in_sem,
    down_sem,
    s_acc,
    r_acc,
    s_ml,
    r_ml,
    s_att,
    r_att,
    s_o,
    r_o,
    s_res,
    r_res,
    s_all,
    r_all,
    s_d,
    r_d,
    s_f,
    r_f,
    s_out,
    r_out,
):
    me = lax.axis_index("blk")
    my_kv = lax.axis_index("kv")
    width = out_ref.shape[1]

    def in_copy(tile):
        return pltpu.make_async_copy(w_in.at[tile // 8, :, lax.rem(tile, 8)], inbuf.at[tile], in_sem.at[tile])

    def down_copy(piece):
        columns = pl.ds(pl.multiple_of(piece * width, width), width)
        return pltpu.make_async_copy(w_down.at[:, columns], downbuf.at[piece], down_sem.at[piece])

    lax.fori_loop(0, 16, lambda tile, c: (in_copy(tile).start(), c)[1], 0)
    lax.fori_loop(0, blk_size, lambda piece, c: (down_copy(piece).start(), c)[1], 0)
    greet((("blk", blk_size), ("kv", kv_size)))

    waits = []
    pairs = []
    for off in range(1, blk_size):
        peer = lax.rem(me + off, blk_size)
        one = push(acc_ref.at[peer], got_acc.at[off - 1], s_acc.at[off - 1], r_acc.at[off - 1], "blk", peer)
        two = push(ml_ref.at[peer // 2], got_ml.at[off - 1], s_ml.at[off - 1], r_ml.at[off - 1], "blk", peer)
        pairs.append((one, two))
        waits += [one, two]
    stats = [ml_ref[me // 2]]
    for off in range(1, blk_size):
        pairs[off - 1][1].wait_recv()
        stats.append(got_ml[off - 1])
    tops = [stat[0:8] for stat in stats]
    best = functools.reduce(jnp.maximum, tops)
    factors = [jnp.exp(top - best) for top in tops]
    total = functools.reduce(jnp.add, [f * stat[8:16] for f, stat in zip(factors, stats)])
    rows = jnp.concatenate([(f / total)[0:1] for f in factors], axis=0)
    coef[...] = jnp.transpose(jnp.concatenate([rows] * 16, axis=0))
    mine = coef[pl.ds(pl.multiple_of(lax.rem(me, 2) * 64, 64), 64), :]
    joint = mine[:, 0:1] * acc_ref[me].astype(jnp.float32)
    for off in range(1, blk_size):
        pairs[off - 1][0].wait_recv()
        joint = joint + mine[:, off : off + 1] * got_acc[off - 1].astype(jnp.float32)
    attended[me] = joint.astype(jnp.bfloat16)
    copies = []
    for off in range(1, blk_size):
        peer = lax.rem(me + off, blk_size)
        copies.append(
            push(attended.at[me], attended.at[me], s_att.at[off - 1], r_att.at[off - 1], "blk", peer)
        )
    for copy in copies:
        copy.wait_recv()
    waits += copies

    heads = []
    for head in range(2):
        blocks = [
            attended[(group * 2 + head) * 2 + half].astype(jnp.float32)
            for half in range(2)
            for group in range(2)
        ]
        for c in range(4):
            rows = []
            for step in range(4):
                for group in range(2):
                    block = blocks[(step // 2) * 2 + group]
                    start = ((step % 2) * 4 + c) * 8
                    rows.append(block[start : start + 8])
            heads.append(jnp.concatenate(rows, axis=0).astype(jnp.bfloat16))
    opart[...] = dot32(jnp.concatenate(heads, axis=1), wo_ref[...]).astype(jnp.bfloat16)

    def step_rows(index):
        return pl.ds(pl.multiple_of(index * 16, 16), 16)

    copies = []
    for off in range(1, kv_size):
        peer = lax.rem(my_kv + off, kv_size)
        copies.append(
            push(opart.at[step_rows(peer)], got_o.at[off - 1], s_o.at[off - 1], r_o.at[off - 1], "kv", peer)
        )
    sums = x_ref[step_rows(my_kv), :].astype(jnp.float32) + opart[step_rows(my_kv), :].astype(jnp.float32)
    for off in range(1, kv_size):
        copies[off - 1].wait_recv()
        sums = sums + got_o[off - 1].astype(jnp.float32)
    waits += copies
    resid[step_rows(my_kv), :] = sums.astype(jnp.bfloat16)
    copies = []
    for off in range(1, kv_size):
        peer = lax.rem(my_kv + off, kv_size)
        copies.append(
            push(
                resid.at[step_rows(my_kv)], resid.at[step_rows(my_kv)], s_res.at[off - 1], r_res.at[off - 1], "kv", peer
            )
        )
    for copy in copies:
        copy.wait_recv()
    waits += copies

    gathered[me] = resid[...]
    core = lax.rem(me, 2)
    partner = me + 1 - 2 * core
    chips = blk_size // 2
    near = push(gathered.at[me], gathered.at[me], s_all.at[0], r_all.at[0], "blk", partner)
    far = []
    for off in range(1, chips):
        peer = lax.rem(me + 2 * off, blk_size)
        far.append(push(gathered.at[me], gathered.at[me], s_all.at[off], r_all.at[off], "blk", peer))
    relays = []
    matrix = spread_matrix()
    stat_rows[...] = jnp.zeros_like(stat_rows)
    logit_rows[...] = jnp.zeros_like(logit_rows)

    def absorb(source, first):
        values = gathered[source].astype(jnp.float32)
        stat_rows[...] += jnp.broadcast_to(jnp.sum(values * values, axis=1, keepdims=True), (64, 128))
        columns = pl.ds(pl.multiple_of(source * width, width), width)
        pre = (values * gain_ref[:, columns].astype(jnp.float32)).astype(jnp.bfloat16)
        logit_rows[...] += dot32_t(pre, router_ref[:, columns])
        spread(pre, matrix, wide, 0)
        rows = pl.ds(pl.multiple_of(source * width, width), width)

        def tile_body(pair, carry):
            tile = pair * 2
            if first:
                in_copy(tile).wait()
                in_copy(tile + 1).wait()
            right = jnp.concatenate(
                [
                    inbuf.at[tile, rows].reshape(2 * width, 128)[...],
                    inbuf.at[tile + 1, rows].reshape(2 * width, 128)[...],
                ],
                axis=1,
            )
            both = dot32(wide[...], right)
            if first:
                sums_in[pair] = both
            else:
                sums_in[pair] += both
            return carry

        lax.fori_loop(0, 8, tile_body, 0)

    def relay(off):
        far[off - 1].wait_recv()
        origin = lax.rem(me + blk_size - 2 * off, blk_size)
        relays.append(
            push(
                gathered.at[origin],
                gathered.at[origin],
                s_all.at[chips - 1 + off],
                r_all.at[chips - 1 + off],
                "blk",
                partner,
            )
        )
        return origin

    absorb(me, True)
    near.wait_recv()
    origins = [relay(off) for off in range(1, chips)]
    absorb(partner, False)
    for origin in origins:
        absorb(origin, False)
    for off in range(1, chips):
        relays[off - 1].wait_recv()
        absorb(lax.rem(partner + blk_size - 2 * off, blk_size), False)
    waits += [near] + far + relays

    inverse = lax.rsqrt(stat_rows[:, 0:1] * (1.0 / MODEL_WIDTH) + NORM_FLOOR)
    logits = logit_rows[...] * inverse
    lane = lax.broadcasted_iota(jnp.int32, (64, EXPERTS), 1)
    pick_one = routes_ref[:, 0:1]
    pick_two = routes_ref[:, 1:2]
    logit_one = jnp.sum(jnp.where(lane == pick_one, logits, 0.0), axis=1, keepdims=True)
    logit_two = jnp.sum(jnp.where(lane == pick_two, logits, 0.0), axis=1, keepdims=True)
    share_one = 1.0 / (1.0 + jnp.exp(logit_two - logit_one))
    share_two = 1.0 / (1.0 + jnp.exp(logit_one - logit_two))
    named = []
    shares = []
    for local in range(2):
        expert = my_kv * 2 + local
        is_one = pick_one == expert
        is_two = pick_two == expert
        named.append(jnp.where(is_one | is_two, 1, 0))
        shares.append(jnp.where(is_one, share_one, jnp.where(is_two, share_two, 0.0)))

    for local in range(2):

        def expert_body(pair, carry, local=local):
            both = sums_in[local * 4 + pair]
            gate = both[:64] * inverse
            up = both[64:] * inverse
            act = gate / (1.0 + jnp.exp(-gate)) * up * shares[local]
            act = jnp.where(named[local] > 0, act, 0.0)
            hidden[:, pl.ds(pl.multiple_of(local * 1024 + pair * 256, 256), 256)] = act.astype(jnp.bfloat16)
            return carry

        lax.fori_loop(0, 4, expert_body, 0)

    copies = []
    mixed = None
    for off in range(1, blk_size + 1):
        peer = lax.rem(me + off, blk_size)
        down_copy(peer).wait()
        piece = dot32(hidden[...], downbuf[peer])
        if off < blk_size:
            dpart[off - 1] = piece.astype(jnp.bfloat16)
            copies.append(
                push(dpart.at[off - 1], got_d.at[off - 1], s_d.at[off - 1], r_d.at[off - 1], "blk", peer)
            )
        else:
            mixed = piece
    for off in range(1, blk_size):
        copies[off - 1].wait_recv()
        mixed = mixed + got_d[off - 1].astype(jnp.float32)
    waits += copies
    fpart[...] = mixed.astype(jnp.bfloat16)
    copies = []
    for off in range(1, kv_size):
        peer = lax.rem(my_kv + off, kv_size)
        copies.append(
            push(fpart.at[step_rows(peer)], got_f.at[off - 1], s_f.at[off - 1], r_f.at[off - 1], "kv", peer)
        )
    sums = resid[step_rows(my_kv), :].astype(jnp.float32) + fpart[step_rows(my_kv), :].astype(jnp.float32)
    for off in range(1, kv_size):
        copies[off - 1].wait_recv()
        sums = sums + got_f[off - 1].astype(jnp.float32)
    waits += copies
    outs[step_rows(my_kv), :] = sums.astype(jnp.bfloat16)
    copies = []
    for off in range(1, kv_size):
        peer = lax.rem(my_kv + off, kv_size)
        copies.append(
            push(
                outs.at[step_rows(my_kv)], outs.at[step_rows(my_kv)], s_out.at[off - 1], r_out.at[off - 1], "kv", peer
            )
        )
    for copy in copies:
        copy.wait_recv()
    waits += copies
    out_ref[...] = outs[...]
    for copy in waits:
        copy.wait_send()


def lookup(table, index):
    slots = jnp.arange(table.shape[0], dtype=jnp.int32)
    return jnp.sum(jnp.where(index[..., None] == slots, table, 0), axis=-1)


def kernel_body(
    blk_size,
    kv_size,
    hidden_in,
    attn_gain,
    ffn_gain,
    query_key_value_weight,
    out_weight,
    router_weight,
    expert_in,
    expert_down,
    kv_cache,
    lengths,
    tables,
    parents,
    routes,
):
    bf16, f32 = jnp.bfloat16, jnp.float32
    vmem = pl.BlockSpec(memory_space=pltpu.VMEM)
    smem = pl.BlockSpec(memory_space=pltpu.SMEM)
    hbm = pl.BlockSpec(memory_space=pl.ANY)
    dma = pltpu.SemaphoreType.DMA
    width = hidden_in.shape[2]
    x = hidden_in.reshape(64, width)
    half = HEAD_WIDTH // 2
    frequency = ROPE_BASE ** (-(jnp.arange(half, dtype=f32) * (2.0 / HEAD_WIDTH)))
    token = jnp.arange(64, dtype=jnp.int32)
    position = lookup(lengths, (token % 16) // BEAM_W) + token // 16
    angle = position.astype(f32)[:, None] * frequency
    cosine, sine_part = jnp.cos(angle), jnp.sin(angle)
    cosine = jnp.concatenate([cosine, cosine], axis=1)
    sine_part = jnp.concatenate([-sine_part, sine_part], axis=1)
    w_qkv = query_key_value_weight.reshape(width, 2, 6, 128).transpose(0, 2, 1, 3)
    qkv = pl.pallas_call(
        functools.partial(project_kernel, blk_size),
        out_shape=jax.ShapeDtypeStruct((blk_size, 6, 16, 128), bf16),
        in_specs=[vmem] * 4 + [hbm],
        out_specs=vmem,
        scratch_shapes=[
            pltpu.VMEM((6, width, 2, 128), bf16),
            pltpu.VMEM((128, 2 * width), bf16),
            pltpu.VMEM((8, 128, 128), bf16),
            pltpu.VMEM((blk_size - 1, 8, 16, 128), bf16),
            dma((6,)),
        ]
        + [dma((blk_size - 1,))] * 4,
        compiler_params=pltpu.CompilerParams(
            collective_id=0, has_side_effects=True, vmem_limit_bytes=24 * 2**20
        ),
        name="project",
    )(x, attn_gain.reshape(1, width), cosine, sine_part, w_qkv)

    steps = jnp.arange(DECODE_STEPS, dtype=jnp.int32)
    current = jnp.broadcast_to(jnp.arange(BEAM_TOTAL, dtype=jnp.int32), (DECODE_STEPS, BEAM_TOTAL))
    chain = [None] * DECODE_STEPS
    for k in range(DECODE_STEPS - 1, -1, -1):
        chain[k] = jnp.where(steps[:, None] >= k, current, -1)
        current = jnp.where(steps[:, None] >= k, lookup(parents[k], current), current)
    anchor = current
    chain = jnp.stack(chain, axis=1)
    by_group = jnp.moveaxis(anchor.reshape(DECODE_STEPS, 2, BEAM_W), 1, 0)
    anchor_rows = jnp.broadcast_to(by_group[:, :, None, :, None], (2, 4, 4, BEAM_W, 128)).reshape(2, 128, 128)
    seen = chain[:, :, :, None] == jnp.arange(BEAM_TOTAL, dtype=jnp.int32)
    seen = jnp.transpose(seen, (0, 2, 1, 3)).reshape(DECODE_STEPS, 2, BEAM_W, 64)
    seen = (seen & (lax.axis_index("blk") == 0)).astype(jnp.int32)
    seen = jnp.pad(jnp.moveaxis(seen, 1, 0), ((0, 0), (0, 0), (0, 0), (0, 64)))
    recent = jnp.broadcast_to(seen[:, :, None], (2, 4, 4, BEAM_W, 128)).reshape(2, 128, 128)

    slot_count = kv_cache.shape[0]
    slots = jnp.arange(slot_count, dtype=jnp.int32)
    flat = tables.reshape(-1)
    entries = jnp.arange(flat.shape[0], dtype=jnp.int32)
    here = (slots + lax.axis_index("blk") * slot_count)[:, None] == flat[None, :]
    entry = jnp.sum(jnp.where(here, entries[None, :], 0), axis=1)
    owner = entry // BEAM_BLOCKS
    start = (entry % BEAM_BLOCKS) * BLOCK_POSITIONS
    group = owner // BEAM_W
    limit = jnp.clip(lookup(lengths, group) - start, 0, BLOCK_POSITIONS)
    used = jnp.any(owner[:, None] == anchor.reshape(1, -1), axis=1)
    live = (limit > 0) & used
    packed = slots + owner * 256 + limit * 8192
    member = live[None, :] & (group[None, :] == jnp.arange(2, dtype=jnp.int32)[:, None])
    before = jnp.sum(member[:, None, :] & (slots[None, :] < slots[:, None])[None], axis=2, dtype=jnp.int32)
    chosen = member[:, None, :] & (before[:, None, :] == slots[None, :, None])
    listing = jnp.sum(jnp.where(chosen, packed[None, None, :], 0), axis=2).reshape(-1)
    counts = jnp.sum(member, axis=1, dtype=jnp.int32)

    acc, stats = pl.pallas_call(
        attend_kernel,
        out_shape=(jax.ShapeDtypeStruct((8, 64, 128), bf16), jax.ShapeDtypeStruct((4, 16, 128), f32)),
        in_specs=[smem, smem, vmem, vmem, vmem, hbm],
        out_specs=(vmem, vmem),
        scratch_shapes=[
            pltpu.VMEM((4, 128, 128), bf16),
            pltpu.VMEM((4, 128, 128), f32),
            pltpu.VMEM((4, 128, 128), f32),
            pltpu.VMEM((4, 128, 128), f32),
            pltpu.VMEM((DEPTH, CHUNK, 2, 2, 128, 128), bf16),
            dma((DEPTH, CHUNK)),
        ],
        compiler_params=pltpu.CompilerParams(vmem_limit_bytes=32 * 2**20),
        name="attend",
    )(listing, counts, qkv, anchor_rows, recent, kv_cache)

    w_in = expert_in.reshape(2, MODEL_WIDTH, 2, 8, 128).transpose(0, 1, 3, 2, 4)
    b, k = blk_size - 1, kv_size - 1
    out = pl.pallas_call(
        functools.partial(layer_kernel, blk_size, kv_size),
        out_shape=jax.ShapeDtypeStruct((64, width), bf16),
        in_specs=[vmem] * 7 + [hbm] * 2,
        out_specs=vmem,
        scratch_shapes=[
            pltpu.VMEM((16, MODEL_WIDTH, 2, 128), bf16),
            pltpu.VMEM((blk_size, 2048, width), bf16),
            pltpu.VMEM((128, 2 * width), bf16),
            pltpu.VMEM((64, 2048), bf16),
            pltpu.VMEM((b, 64, 128), bf16),
            pltpu.VMEM((b, 16, 128), f32),
            pltpu.VMEM((128, 128), f32),
            pltpu.VMEM((blk_size, 64, 128), bf16),
            pltpu.VMEM((64, width), bf16),
            pltpu.VMEM((k, 16, width), bf16),
            pltpu.VMEM((64, width), bf16),
            pltpu.VMEM((blk_size, 64, width), bf16),
            pltpu.VMEM((b, 64, width), bf16),
            pltpu.VMEM((b, 64, width), bf16),
            pltpu.VMEM((64, width), bf16),
            pltpu.VMEM((k, 16, width), bf16),
            pltpu.VMEM((64, width), bf16),
            pltpu.VMEM((8, 128, 256), f32),
            pltpu.VMEM((64, 128), f32),
            pltpu.VMEM((64, EXPERTS), f32),
            dma((16,)),
            dma((blk_size,)),
        ]
        + [dma((b,))] * 6
        + [dma((k,))] * 4
        + [dma((b,))] * 4
        + [dma((k,))] * 4,
        compiler_params=pltpu.CompilerParams(
            collective_id=1, has_side_effects=True, vmem_limit_bytes=60 * 2**20
        ),
        name="layer",
    )(
        acc,
        stats,
        x,
        out_weight,
        ffn_gain.reshape(1, MODEL_WIDTH),
        router_weight.T,
        routes.reshape(64, 2),
        w_in,
        expert_down.reshape(2048, MODEL_WIDTH),
    )
    return out.reshape(DECODE_STEPS, BEAM_TOTAL, width)


def solution(mesh):
    blk_size, kv_size = mesh.shape["blk"], mesh.shape["kv"]
    if (blk_size, kv_size) == (8, 4):
        run = functools.partial(kernel_body, blk_size, kv_size)
    else:
        run = body
    placed = (
        P(None, None, "blk"),
        P("blk"),
        P(),
        P("blk", "kv", None),
        P("kv", "blk"),
        P(),
        P("kv", None, None, "blk"),
        P("kv", "blk", None),
        P("blk", None, "kv", None, None),
        P(),
        P(),
        P(),
        P(),
    )
    return jax.shard_map(
        run, mesh=mesh, in_specs=placed, out_specs=P(None, None, "blk"), check_vma=False
    )
```
